512 devices in a mesh: test: 8 (over z_lo, core), slab: 64 (over y, x, z_hi).
Axes of the slice: x: 4, y: 4, z: 16 (z_hi: 4, z_lo: 4; z = z_hi * 4 + z_lo), core: 2. Of those that a mesh axis runs over, the one named last changes fastest.
Arguments:
- log_conductivity: float32 [128, 512, 128], P('slab'), may hold values from -4 to 4
- storage: float32 [128, 512, 128], P('slab'), may hold values from 0.1 to 1
- active_mask: int32 [128, 512, 128], P('slab'), may hold values 0 or 1
- heads: float32 [8, 128, 512, 128], P('test', 'slab'), may hold values from -6 to 6
- adjoint_next: float32 [8, 128, 512, 128], P('test', 'slab'), may hold values from -6 to 6
- pump_cells: int32 [8], P('test'), may hold values from 0 to 8388607
- obs_cells: int32 [64], replicated, may hold values from 0 to 8388607
- obs_data: float32 [8, 64], P('test'), may hold values from -6 to 6
Outputs:
- adjoint: float32 [8, 128, 512, 128], P('test', 'slab')
- gradient: float32 [128, 512, 128], P('slab')
The draws below stay inside these ranges and needn't reach their ends.
All inputs are finite; a program needn't handle non-finite values. No bound on the sum of `active_mask` on one device may be relied on, other than what follows from the above.
Results may differ from the reference program's by a relative error of at most 0.0003.
Values sent between devices are 32-bit elements; how exact they have to be, the bound alone decides.
A program may use at most 64 MiB of HBM per device.

```python
import math
import jax
import jax.numpy as jnp
from jax import lax

NY = 512
NZ = 128
NOBS = 64
ITERS = 3
TESTS = 8
NX = 128


def axis_wave(key_length, key_phase, extent):
    wave_length = jax.random.uniform(key_length, (TESTS, 4), jnp.float32, 16.0, 48.0)
    wave_phase = jax.random.uniform(key_phase, (TESTS, 4), jnp.float32, -math.pi, math.pi)
    position = jnp.arange(extent, dtype=jnp.float32)
    number = 2.0 * math.pi / wave_length
    return jnp.cos(number[:, :, None] * position[None, None, :] + wave_phase[:, :, None])


def draw_adjoint_next(key, part):
    subkeys = jax.random.split(key, 8)
    waves_x = axis_wave(subkeys[0], subkeys[1], NX)
    waves_y = axis_wave(subkeys[2], subkeys[3], NY)
    waves_z = axis_wave(subkeys[4], subkeys[5], NZ)
    amplitude = jax.random.uniform(subkeys[6], (TESTS, 4), jnp.float32, 0.9, 1.3)
    smooth = jnp.zeros((TESTS, NX, NY, NZ), jnp.float32)
    for which in range(4):
        smooth = smooth + amplitude[:, which, None, None, None] * waves_x[:, which, :, None, None] * waves_y[:, which, None, :, None] * waves_z[:, which, None, None, :]
    noise = 0.1 * jnp.clip(jax.random.normal(subkeys[7], (TESTS, NX, NY, NZ), jnp.float32), -3.0, 3.0)
    return smooth + noise


def plant(values, own_key, smallest, high):
    place = [jax.random.randint(jax.random.fold_in(own_key, axis), (), 0, length) for axis, length in enumerate(values.shape)]
    longest = values.shape.index(max(values.shape))
    next_to = place[:longest] + [(place[longest] + 1) % values.shape[longest]] + place[longest + 1:]
    return values.at[tuple(place)].set(smallest).at[tuple(next_to)].set(high)


def block_scale(own_key, shape, cuts, least, top_value):
    loudness, own = 1.0, jax.random.fold_in(own_key, 6)
    for axis_at, parts in cuts:
        draws = jnp.exp(jax.random.uniform(jax.random.fold_in(own, axis_at), (parts,), jnp.float32, least / len(cuts), top_value / len(cuts)))
        loudness = loudness * jnp.repeat(draws, shape[axis_at] // parts).reshape([-1 if axis == axis_at else 1 for axis in range(len(shape))])
    return loudness


def scatter_about(own_key, shape, width, bound, pieces=(), held_as=jnp.bfloat16):
    gain = block_scale(own_key, shape, pieces, -0.22, 0.18) if pieces else 1.0
    array = jax.random.normal(own_key, shape, jnp.float32) * width * gain
    return jnp.minimum(jnp.maximum(array, -bound), bound).astype(held_as)


def setup_inputs(seed: int = 0) -> dict:
    streams_of = jax.random.split(jax.random.key(seed), 9)
    log_conductivity = scatter_about(streams_of[0], (NX, NY, NZ), 1.0, 4.0, ((0, 64),), jnp.float32)
    storage = jnp.clip(jnp.exp(math.log(1.0) - 2.3025851 * jax.random.uniform(streams_of[1], (NX, NY, NZ), jnp.float32) ** block_scale(streams_of[1], (NX, NY, NZ), ((0, 64),), -0.2, 0.2)), 0.1, 1.0)
    active_mask = plant((jax.random.randint(streams_of[2], (NX, NY, NZ), 0, 8) < 7).astype(jnp.int32), jax.random.fold_in(streams_of[2], 1), 0, 1)
    heads = scatter_about(streams_of[3], (TESTS, NX, NY, NZ), 1.0, 6.0, ((0, 8), (1, 64)), jnp.float32)
    adjoint_next = draw_adjoint_next(jax.random.fold_in(streams_of[8], 71), 0)
    pump_cells = plant(jax.random.randint(streams_of[5], (TESTS,), 0, NX * NY * NZ), jax.random.fold_in(streams_of[5], 1), 0, (NX * NY * NZ) - 1).astype(jnp.int32)
    obs_cells = plant(jax.random.randint(streams_of[6], (NOBS,), 0, NX * NY * NZ), jax.random.fold_in(streams_of[6], 1), 0, (NX * NY * NZ) - 1).astype(jnp.int32)
    obs_data = scatter_about(streams_of[7], (TESTS, NOBS), 1.0, 6.0, ((0, 8),), jnp.float32)
    return {"log_conductivity": log_conductivity, "storage": storage, "active_mask": active_mask, "heads": heads, "adjoint_next": adjoint_next, "pump_cells": pump_cells, "obs_cells": obs_cells, "obs_data": obs_data}


WELL_TERM = 4.0


def part_of(v, axis_num, start, length):
    return lax.slice_in_dim(v, start, start + length, axis=axis_num)


def pad_axis(v, axis_num):
    widths = [(0, 0)] * v.ndim
    widths[axis_num] = (1, 1)
    return jnp.pad(v, widths)


def face_values(cond_pad, axis_num):
    count = cond_pad.shape[axis_num] - 1
    left = part_of(cond_pad, axis_num, 0, count)
    right = part_of(cond_pad, axis_num, 1, count)
    return 2.0 * left * right / (left + right)


def flux_axis(padded, faces, axis_num):
    count = padded.shape[axis_num] - 1
    terms = faces * (part_of(padded, axis_num, 0, count) - part_of(padded, axis_num, 1, count))
    return part_of(terms, axis_num, 1, count - 1) - part_of(terms, axis_num, 0, count - 1)


def face_total(faces, axis_num):
    count = faces.shape[axis_num] - 1
    return part_of(faces, axis_num, 1, count) + part_of(faces, axis_num, 0, count)


def operate(field, field_x, faces, self_term, active):
    flux = flux_axis(field_x, faces[0], 0)
    flux = flux + flux_axis(pad_axis(field, 1), faces[1], 1)
    flux = flux + flux_axis(pad_axis(field, 2), faces[2], 2)
    return active * (self_term * field + flux) + (1.0 - active) * field


def slope(own, other):
    total = own + other
    return 2.0 * own * other * other / (total * total)


def side_terms(cond_pad, adj_pad, head_pad, axis_num):
    count = cond_pad.shape[axis_num] - 2
    cond_c = part_of(cond_pad, axis_num, 1, count)
    adj_c = part_of(adj_pad, axis_num, 1, count)
    head_c = part_of(head_pad, axis_num, 1, count)
    total = jnp.zeros(cond_c.shape, jnp.float32)
    for start in (0, 2):
        cond_n = part_of(cond_pad, axis_num, start, count)
        adj_n = part_of(adj_pad, axis_num, start, count)
        head_n = part_of(head_pad, axis_num, start, count)
        total = total + slope(cond_c, cond_n) * (adj_c - adj_n) * (head_c - head_n)
    return total


def reference(log_conductivity, storage, active_mask, heads, adjoint_next, pump_cells, obs_cells, obs_data):
    conduct = jnp.exp(log_conductivity)
    active = active_mask.astype(jnp.float32)
    faces = tuple(face_values(pad_axis(conduct, a), a) for a in range(3))
    face_sum = face_total(faces[0], 0) + face_total(faces[1], 1) + face_total(faces[2], 2)
    cond_pads = tuple(pad_axis(conduct, a) for a in range(3))

    def one_test(items):
        heads_t, later_t, pump_t, data_t = items
        well = jnp.zeros((NX * NY * NZ,), jnp.float32).at[pump_t].set(WELL_TERM).reshape(NX, NY, NZ)
        self_term = storage + well
        diag = active * (self_term + face_sum) + (1.0 - active)
        values = heads_t.reshape(-1)[obs_cells] - data_t
        misfit = jnp.zeros((NX * NY * NZ,), jnp.float32).at[obs_cells].add(values).reshape(NX, NY, NZ)
        rhs = active * (storage * later_t + misfit)
        solution = jnp.zeros_like(rhs)
        resid = rhs
        precond = resid / diag
        direction = precond
        rz_now = jnp.sum(resid * precond)
        for step in range(ITERS):
            image = operate(direction, pad_axis(direction, 0), faces, self_term, active)
            alpha = rz_now / jnp.sum(direction * image)
            solution = solution + alpha * direction
            resid = resid - alpha * image
            precond = resid / diag
            rz_next = jnp.sum(resid * precond)
            direction = precond + (rz_next / rz_now) * direction
            rz_now = rz_next
        terms = jnp.zeros_like(rhs)
        for a in range(3):
            terms = terms + side_terms(cond_pads[a], pad_axis(solution, a), pad_axis(heads_t, a), a)
        return solution, -terms

    adjoint, grads = lax.map(one_test, (heads, adjoint_next, pump_cells, obs_data))
    gradient = jnp.sum(grads, axis=0)
    return adjoint, gradient
```

```python
import functools

import jax
import jax.numpy as jnp
from jax import lax
from jax.experimental import pallas as pl
from jax.experimental.pallas import tpu as pltpu
from jax.sharding import PartitionSpec as P

MESH = pl.DeviceIdType.MESH
WELL_TERM = 4.0
SLABS = 64
ROWS = 512
LANES = 128
NOBS = 64
PAD = 8
BLOCK = 16
CHUNK = 128
CHUNKS = ROWS // CHUNK
HALF = ROWS // 2
PIECE = 64


class Copies:
    def __init__(self, send, recv):
        self.send, self.recv, self.count = send, recv, 0

    def start(self, src, dst, **where):
        copy = pltpu.make_async_remote_copy(
            src_ref=src,
            dst_ref=dst,
            send_sem=self.send.at[self.count],
            recv_sem=self.recv.at[self.count],
            device_id=where,
            device_id_type=MESH,
        )
        self.count += 1
        copy.start()
        return copy


N_COPIES = 2 + 4 + 2 + 2 * CHUNKS + 2 * CHUNKS + CHUNKS + 3 * 18 + 1 + 3 + 1 + 4


def rows_at(start, size=BLOCK):
    return pl.ds(start, size)


def kernel(
    lk, sto, act_in, hd, adj, pump, obs_col, obs_row, obs_val, adj_out, grad_out,
    kpad, hpad, zpad, lpad, klog, krim, faces, slopes, rim_coef, self_t, diag, inv, rhs,
    p_now, g0, g1, y1, z0r, g0r, z1r, g1r, hrim, msg, inbox, gpart, pair_in, gsum, piece_in, gfull,
    far_in, send, recv,
):
    me = lax.axis_index("slab")
    test = lax.axis_index("test")
    above, below = lax.rem(me + 1, SLABS), lax.rem(me + SLABS - 1, SLABS)
    chip, core = test // 2, lax.rem(test, 2)
    sibling = test + 1 - 2 * core
    mates = [lax.rem(test + 2 * i, 8) for i in (1, 2, 3)]
    plane_at, deep = me // 4, lax.rem(me, 4)
    col, line = lax.rem(plane_at, 4), plane_at // 4
    z_part = [plane_at * 4 + lax.rem(deep + i, 4) for i in (1, 2, 3)]
    xy_part = [
        (lax.rem(line + j, 4) * 4 + lax.rem(col + i, 4)) * 4 + deep
        for j in range(4) for i in range(4) if i or j
    ]
    barrier = pltpu.get_barrier_semaphore()
    for other in [above, below] + z_part + xy_part:
        pl.semaphore_signal(barrier, inc=1, device_id={"slab": other}, device_id_type=MESH)
    for other in [sibling] + mates:
        pl.semaphore_signal(barrier, inc=1, device_id={"test": other}, device_id_type=MESH)
    copies = Copies(send, recv)
    pending = []

    def begin(src, dst, **where):
        copy = copies.start(src, dst, **where)
        pending.append(copy)
        return copy

    own = pl.ds(pl.multiple_of(core * HALF + chip * PIECE, PIECE), PIECE)
    own_half = pl.ds(pl.multiple_of(core * HALF, HALF), HALF)

    pl.semaphore_wait(barrier, 24)
    to_above = begin(lk.at[1, own], klog.at[0, own], slab=above)
    to_below = begin(lk.at[0, own], klog.at[1, own], slab=below)
    head_copies = [
        begin(hd.at[1, pl.ds(0, HALF)], hrim.at[pl.ds(0, HALF)], slab=above),
        begin(hd.at[0, pl.ds(HALF, HALF)], hrim.at[pl.ds(HALF, HALF)], slab=below),
    ]

    low_pad = jnp.zeros((2, PAD, LANES), jnp.float32)
    for ref, fill in ((kpad, 1.0), (hpad, 0.0), (zpad, 0.0), (lpad, 0.0)):
        ref[:, pl.ds(0, PAD), :] = low_pad + fill
        ref[:, pl.ds(PAD + ROWS, PAD), :] = low_pad + fill

    offset = me * (2 * ROWS)
    cell_row = obs_col[...] // LANES - offset
    cell_lane = lax.rem(obs_col[...], LANES)
    hit = lax.broadcasted_iota(jnp.int32, (NOBS, LANES), 1) == cell_lane
    picked = jnp.zeros((NOBS, LANES), jnp.float32)
    for x in range(2):
        where_row = lax.broadcasted_iota(jnp.int32, (NOBS, ROWS), 1) + x * ROWS == cell_row
        picked = picked + jnp.dot(
            where_row.astype(jnp.float32), hd[x],
            precision=lax.Precision.HIGHEST, preferred_element_type=jnp.float32,
        )
    values = jnp.where(hit, picked - obs_val[...], 0.0)
    row_of = obs_row[...] // LANES - offset
    for x in range(2):
        where_row = lax.broadcasted_iota(jnp.int32, (ROWS, NOBS), 0) + x * ROWS == row_of
        rhs[x] = jnp.dot(
            where_row.astype(jnp.float32), values,
            precision=lax.Precision.HIGHEST, preferred_element_type=jnp.float32,
        )

    well_at = pump[0] - offset * LANES
    shape = (2, BLOCK, LANES)
    lane_no = lax.broadcasted_iota(jnp.int32, shape, 2)
    row_no = lax.broadcasted_iota(jnp.int32, shape, 1)
    cell_no = lax.broadcasted_iota(jnp.int32, shape, 0) * (ROWS * LANES) + row_no * LANES + lane_no

    def prepare(i, carry):
        at = pl.multiple_of(i * BLOCK, BLOCK)
        here = rows_at(at)
        kpad[:, rows_at(pl.multiple_of(PAD + at, 8)), :] = jnp.exp(lk[:, here, :])
        hpad[:, rows_at(pl.multiple_of(PAD + at, 8)), :] = hd[:, here, :]
        return carry

    lax.fori_loop(0, ROWS // BLOCK, prepare, 0)

    def local_terms(i, carry):
        at = pl.multiple_of(i * BLOCK, BLOCK)
        here = rows_at(at)
        k = kpad[:, rows_at(pl.multiple_of(PAD + at, 8)), :]
        total = jnp.zeros(shape, jnp.float32)
        sides = (
            (kpad[:, rows_at(PAD - 1 + at), :], row_no + at > 0),
            (kpad[:, rows_at(PAD + 1 + at), :], row_no + at < ROWS - 1),
            (pltpu.roll(k, 1, 2), lane_no > 0),
            (pltpu.roll(k, LANES - 1, 2), lane_no < LANES - 1),
        )
        for n, (other, inside) in enumerate(sides):
            both = k + other
            face = jnp.where(inside, 2.0 * k * other / both, 0.0)
            faces[n, :, here, :] = face
            slopes[n, :, here, :] = face * other / both
            total = total + face
        both = k[0] + k[1]
        face = 2.0 * k[0] * k[1] / both
        rim_coef[0, here, :] = face
        rim_coef[1, here, :] = face * k[1] / both
        rim_coef[2, here, :] = face * k[0] / both
        well = jnp.where(cell_no + at * LANES == well_at, WELL_TERM, 0.0)
        self_here = sto[:, here, :] + well
        self_t[:, here, :] = self_here
        diag[:, here, :] = self_here + total + face[None]
        active = act_in[:, here, :].astype(jnp.float32)
        rhs[:, here, :] = active * (sto[:, here, :] * adj[:, here, :] + rhs[:, here, :])
        return carry

    lax.fori_loop(0, ROWS // BLOCK, local_terms, 0)

    def gather(ref, arrived):
        for copy in arrived:
            copy.wait_recv()
        around = [begin(ref.at[:, own], ref.at[:, own], test=mate) for mate in mates]
        for copy in around:
            copy.wait_recv()
        begin(ref.at[:, own_half], ref.at[:, own_half], test=sibling).wait_recv()

    gather(klog, [to_above, to_below])

    low_edge = jnp.where(me > 0, 1.0, 0.0)
    high_edge = jnp.where(me < SLABS - 1, 1.0, 0.0)

    def rim_terms(i, carry):
        at = pl.multiple_of(i * BLOCK, BLOCK)
        here = rows_at(at)
        k = kpad[:, rows_at(pl.multiple_of(PAD + at, 8)), :]
        other = jnp.exp(klog[:, here, :])
        krim[:, here, :] = other
        both = k + other
        face = 2.0 * k * other / both
        low = face[0] * low_edge
        high = face[1] * high_edge
        rim_coef[3, here, :] = low
        rim_coef[4, here, :] = high
        rim_coef[5, here, :] = low * other[0] / both[0]
        rim_coef[6, here, :] = high * other[1] / both[1]
        rim_coef[7, here, :] = low * k[0] / both[0]
        rim_coef[8, here, :] = high * k[1] / both[1]
        active = act_in[:, here, :].astype(jnp.float32)
        fixed = 1.0 - active
        d0 = active[0] * (diag[0, here, :] + low) + fixed[0]
        d1 = active[1] * (diag[1, here, :] + high) + fixed[1]
        diag[0, here, :] = d0
        diag[1, here, :] = d1
        inv[0, here, :] = 1.0 / d0
        inv[1, here, :] = 1.0 / d1
        there = rows_at(pl.multiple_of(PAD + at, 8))
        z0 = rhs[0, here, :] / d0
        z1 = rhs[1, here, :] / d1
        zpad[0, there, :] = z0
        zpad[1, there, :] = z1
        p_now[0, here, :] = z0
        p_now[1, here, :] = z1
        return carry

    def send_rims(ref, pad, rims, chunk):
        src = pl.ds(pad + chunk * CHUNK, CHUNK)
        dst = pl.ds(chunk * CHUNK, CHUNK)
        return [
            begin(ref.at[1, src], rims.at[0, dst], slab=above),
            begin(ref.at[0, src], rims.at[1, dst], slab=below),
        ]

    per_chunk = CHUNK // BLOCK
    z_copies = []
    for chunk in range(CHUNKS):
        lax.fori_loop(chunk * per_chunk, (chunk + 1) * per_chunk, rim_terms, 0)
        z_copies.append(send_rims(zpad, PAD, z0r, chunk))

    def image_of(at, rim_low, rim_high):
        here = rows_at(at)
        there = rows_at(pl.multiple_of(PAD + at, 8))
        z = zpad[:, there, :]
        flux = faces[0, :, here, :] * (z - zpad[:, rows_at(PAD - 1 + at), :])
        flux = flux + faces[1, :, here, :] * (z - zpad[:, rows_at(PAD + 1 + at), :])
        flux = flux + faces[2, :, here, :] * (z - pltpu.roll(z, 1, 2))
        flux = flux + faces[3, :, here, :] * (z - pltpu.roll(z, LANES - 1, 2))
        across = rim_coef[0, here, :] * (z[0] - z[1])
        low = across + rim_coef[3, here, :] * (z[0] - rim_low)
        high = rim_coef[4, here, :] * (z[1] - rim_high) - across
        active = act_in[:, here, :].astype(jnp.float32)
        body = self_t[:, here, :] * z + flux
        image0 = active[0] * (body[0] + low) + (1.0 - active[0]) * z[0]
        image1 = active[1] * (body[1] + high) + (1.0 - active[1]) * z[1]
        return z, image0, image1

    zero = jnp.zeros((BLOCK, LANES), jnp.float32)

    def inner_terms(sums, z, image0, image1, d):
        rz = sums[0] + z[0] * z[0] * d[0] + z[1] * z[1] * d[1]
        pw = sums[1] + z[0] * image0 + z[1] * image1
        return rz, pw

    def all_sum(which, sums):
        first = jnp.concatenate([jnp.sum(s, axis=0, keepdims=True) for s in sums], axis=0)
        n = 0
        for stage in (z_part, xy_part):
            msg[which, n] = first
            batch = [
                begin(msg.at[which, n], inbox.at[which, n + i], slab=other)
                for i, other in enumerate(stage)
            ]
            for copy in batch:
                copy.wait_recv()
            for i in range(len(stage)):
                first = first + inbox[which, n + i]
            n += len(stage)
        total = jnp.sum(first, axis=1, keepdims=True)
        total = jnp.broadcast_to(total, (2, LANES))
        return total[0:1], total[1:2]

    def first_image(i, sums):
        at = pl.multiple_of(i * BLOCK, BLOCK)
        here = rows_at(at)
        z, image0, image1 = image_of(at, z0r[0, here, :], z0r[1, here, :])
        g0[0, here, :] = image0 * inv[0, here, :]
        g0[1, here, :] = image1 * inv[1, here, :]
        return inner_terms(sums, z, image0, image1, diag[:, here, :])

    sums = (zero, zero)
    g0_copies = []
    for chunk in range(CHUNKS):
        for copy in z_copies[chunk]:
            copy.wait_recv()
        sums = lax.fori_loop(chunk * per_chunk, (chunk + 1) * per_chunk, first_image, sums)
        g0_copies.append(send_rims(g0, 0, g0r, chunk))
    for pairs in z_copies:
        for copy in pairs:
            copy.wait_send()
    done = [id(copy) for pairs in z_copies for copy in pairs]
    pending[:] = [copy for copy in pending if id(copy) not in done]
    rz0, pw0 = all_sum(0, sums)
    alpha0 = rz0 / pw0

    def step_one(i, carry):
        at = pl.multiple_of(i * BLOCK, BLOCK)
        here = rows_at(at)
        zpad[:, rows_at(pl.multiple_of(PAD + at, 8)), :] = p_now[:, here, :] - alpha0 * g0[:, here, :]
        return carry

    lax.fori_loop(0, ROWS // BLOCK, step_one, 0)

    def second_image(i, sums):
        at = pl.multiple_of(i * BLOCK, BLOCK)
        here = rows_at(at)
        rim = z0r[:, here, :] - alpha0 * g0r[:, here, :]
        z1r[:, here, :] = rim
        z, image0, image1 = image_of(at, rim[0], rim[1])
        g1[0, here, :] = image0 * inv[0, here, :]
        g1[1, here, :] = image1 * inv[1, here, :]
        return inner_terms(sums, z, image0, image1, diag[:, here, :])

    sums = (zero, zero)
    g1_copies = []
    for chunk in range(CHUNKS):
        for copy in g0_copies[chunk]:
            copy.wait_recv()
        sums = lax.fori_loop(chunk * per_chunk, (chunk + 1) * per_chunk, second_image, sums)
        part = pl.ds(chunk * CHUNK, CHUNK)
        if chunk < CHUNKS // 2:
            g1_copies.append(begin(g1.at[1, part], g1r.at[part], slab=above))
        else:
            g1_copies.append(begin(g1.at[0, part], g1r.at[part], slab=below))
    rz1, delta1 = all_sum(1, sums)
    beta0 = rz1 / rz0
    alpha1 = rz1 / (delta1 - beta0 * rz1 / alpha0)

    def step_two(i, carry):
        at = pl.multiple_of(i * BLOCK, BLOCK)
        here = rows_at(at)
        there = rows_at(pl.multiple_of(PAD + at, 8))
        z = zpad[:, there, :]
        p0 = p_now[:, here, :]
        p1 = z + beta0 * p0
        lpad[:, there, :] = alpha0 * p0 + alpha1 * p1
        p_now[:, here, :] = p1
        zpad[:, there, :] = z - alpha1 * (g1[:, here, :] + beta0 * g0[:, here, :])
        return carry

    lax.fori_loop(0, ROWS // BLOCK, step_two, 0)

    def energy(side, i, sums):
        at = pl.multiple_of(i * BLOCK, BLOCK)
        here = rows_at(at)
        z = zpad[:, rows_at(pl.multiple_of(PAD + at, 8)), :]
        z0 = z0r[side, here, :]
        z1 = z1r[side, here, :]
        p1 = z1 + beta0 * z0
        rim = z1 - alpha1 * (g1r[here, :] + beta0 * g0r[side, here, :])
        y1[0, here, :] = rim
        y1[1, here, :] = p1
        z1r[side, here, :] = alpha0 * z0 + alpha1 * p1
        up = z - zpad[:, rows_at(PAD + 1 + at), :]
        right = z - pltpu.roll(z, LANES - 1, 2)
        across = z[0] - z[1]
        over = z[side] - rim
        square = faces[1, :, here, :] * up * up + faces[3, :, here, :] * right * right
        square = square + self_t[:, here, :] * z * z
        active = act_in[:, here, :].astype(jnp.float32)
        fixed = (1.0 - active) * z * z
        square = square + fixed
        pw = sums[1] + square[0] + square[1] + rim_coef[0, here, :] * across * across
        pw = pw + rim_coef[3 + side, here, :] * over * over
        d = diag[:, here, :]
        rz = sums[0] + z[0] * z[0] * d[0] + z[1] * z[1] * d[1]
        return rz, pw

    sums = (zero, zero)
    for chunk in range(CHUNKS):
        g1_copies[chunk].wait_recv()
        side = 0 if chunk < CHUNKS // 2 else 1
        sums = lax.fori_loop(
            chunk * per_chunk, (chunk + 1) * per_chunk, functools.partial(energy, side), sums
        )
    rz2, delta2 = all_sum(2, sums)
    beta1 = rz2 / rz1
    alpha2 = rz2 / (delta2 - beta1 * rz2 / alpha1)

    def last_step(i, carry):
        at = pl.multiple_of(i * BLOCK, BLOCK)
        here = rows_at(at)
        there = rows_at(pl.multiple_of(PAD + at, 8))
        new = lpad[:, there, :] + alpha2 * (zpad[:, there, :] + beta1 * p_now[:, here, :])
        lpad[:, there, :] = new
        adj_out[:, here, :] = new
        return carry

    lax.fori_loop(0, ROWS // BLOCK, last_step, 0)

    for copy in head_copies:
        copy.wait_recv()

    def gradient(side, i, carry):
        at = pl.multiple_of(i * BLOCK, BLOCK)
        here = rows_at(at)
        there = rows_at(pl.multiple_of(PAD + at, 8))
        lam = lpad[:, there, :]
        head = hpad[:, there, :]
        lower, upper = rows_at(PAD - 1 + at), rows_at(PAD + 1 + at)
        total = slopes[0, :, here, :] * (lam - lpad[:, lower, :]) * (head - hpad[:, lower, :])
        total = total + slopes[1, :, here, :] * (lam - lpad[:, upper, :]) * (head - hpad[:, upper, :])
        for n, turn in ((2, 1), (3, LANES - 1)):
            total = total + slopes[n, :, here, :] * (lam - pltpu.roll(lam, turn, 2)) * (
                head - pltpu.roll(head, turn, 2)
            )
        across = (lam[0] - lam[1]) * (head[0] - head[1])
        rim = z1r[side, here, :] + alpha2 * (y1[0, here, :] + beta1 * y1[1, here, :])
        over = (lam[side] - rim) * (head[side] - hrim[here, :])
        total0 = total[0] + rim_coef[1, here, :] * across
        total1 = total[1] + rim_coef[2, here, :] * across
        if side == 0:
            total0 = total0 + rim_coef[5, here, :] * over
        else:
            total1 = total1 + rim_coef[6, here, :] * over
        gpart[0, here, :] = -total0
        gpart[1, here, :] = -total1
        gpart[2, here, :] = -rim_coef[7 + side, here, :] * over
        return carry

    blocks = HALF // BLOCK
    lax.fori_loop(0, blocks, functools.partial(gradient, 0), 0)
    lax.fori_loop(blocks, 2 * blocks, functools.partial(gradient, 1), 0)

    other_half = pl.ds(pl.multiple_of((1 - core) * HALF, HALF), HALF)
    begin(gpart.at[:, other_half], pair_in, test=sibling).wait_recv()
    gsum[...] = gpart[:, own_half, :] + pair_in[...]
    spread = []
    for i, mate in enumerate(mates):
        quarter = pl.ds(pl.multiple_of(lax.rem(chip + i + 1, 4) * PIECE, PIECE), PIECE)
        spread.append(begin(gsum.at[:, quarter], piece_in.at[i], test=mate))
    for copy in spread:
        copy.wait_recv()
    quarter = pl.ds(pl.multiple_of(chip * PIECE, PIECE), PIECE)
    piece = gsum[:, quarter, :] + piece_in[0] + piece_in[1] + piece_in[2]
    far_in[0] = piece[2]
    toward = jnp.where(core == 0, below, above)
    begin(far_in.at[0], far_in.at[1], slab=toward).wait_recv()
    gets_low = jnp.where(core == 0, 0.0, 1.0)
    gfull[0, own, :] = piece[0] + gets_low * far_in[1]
    gfull[1, own, :] = piece[1] + (1.0 - gets_low) * far_in[1]
    gather(gfull, [])
    grad_out[...] = gfull[...]
    for copy in pending:
        copy.wait_send()


def on_device(
    log_conductivity, storage, active_mask, heads, adjoint_next, pump_cells, obs_cells, obs_data
):
    full = (2, ROWS, LANES)
    one = (ROWS, LANES)
    padded = (2, ROWS + 2 * PAD, LANES)
    f32 = lambda *s: pltpu.VMEM(s, jnp.float32)
    vmem = pl.BlockSpec(memory_space=pltpu.VMEM)
    adjoint, gradient = pl.pallas_call(
        kernel,
        out_shape=[jax.ShapeDtypeStruct(full, jnp.float32)] * 2,
        in_specs=[vmem] * 5 + [pl.BlockSpec(memory_space=pltpu.SMEM)] + [vmem] * 3,
        out_specs=[vmem] * 2,
        scratch_shapes=[
            f32(*padded), f32(*padded), f32(*padded), f32(*padded),
            f32(*full), f32(*full), f32(4, *full), f32(4, *full), f32(9, *one),
            f32(*full), f32(*full), f32(*full), f32(*full),
            f32(*full), f32(*full), f32(*full), f32(*full),
            f32(*full), f32(*full), f32(*full), f32(*one), f32(*one),
            f32(3, 18, 2, LANES), f32(3, 18, 2, LANES),
            f32(3, *one), f32(3, HALF, LANES), f32(3, HALF, LANES), f32(3, 3, PIECE, LANES), f32(*full),
            f32(2, PIECE, LANES),
            pltpu.SemaphoreType.DMA((N_COPIES,)),
            pltpu.SemaphoreType.DMA((N_COPIES,)),
        ],
        compiler_params=pltpu.CompilerParams(
            collective_id=0, has_side_effects=True, vmem_limit_bytes=56 << 20
        ),
    )(
        log_conductivity, storage, active_mask, heads[0], adjoint_next[0], pump_cells,
        obs_cells.reshape(NOBS, 1), obs_cells.reshape(1, NOBS), obs_data.reshape(NOBS, 1),
    )
    return adjoint[None], gradient


def solution(mesh):
    return jax.shard_map(
        on_device,
        mesh=mesh,
        in_specs=(
            P("slab", None, None),
            P("slab", None, None),
            P("slab", None, None),
            P("test", "slab", None, None),
            P("test", "slab", None, None),
            P("test"),
            P(),
            P("test", None),
        ),
        out_specs=(P("test", "slab", None, None), P("slab", None, None)),
        check_vma=False,
    )
```

```python
import functools

import jax
import jax.numpy as jnp
from jax import lax
from jax.experimental import pallas as pl
from jax.experimental.pallas import tpu as pltpu
from jax.sharding import PartitionSpec as P

MESH = pl.DeviceIdType.MESH
WELL_TERM = 4.0
SLABS = 64
ROWS = 512
LANES = 128
NOBS = 64
PAD = 8
BLOCK = 16
CHUNK = 128
CHUNKS = ROWS // CHUNK
HALF = ROWS // 2
PIECE = 64


class Copies:
    def __init__(self, send, recv):
        self.send, self.recv, self.count = send, recv, 0

    def start(self, src, dst, **where):
        copy = pltpu.make_async_remote_copy(
            src_ref=src,
            dst_ref=dst,
            send_sem=self.send.at[self.count],
            recv_sem=self.recv.at[self.count],
            device_id=where,
            device_id_type=MESH,
        )
        self.count += 1
        copy.start()
        return copy


ORDER = (0, 2, 1, 3)
EARLY = 64
N_COPIES = 2 + 4 + 4 + 2 * CHUNKS + 2 * CHUNKS + CHUNKS + 3 * 18 + 2 + 6 + 1 + 8


def rows_at(start, size=BLOCK):
    return pl.ds(start, size)


def kernel(
    lk_hbm, sto_hbm, act_hbm, hd_hbm, adj_hbm, pump_hbm, cells_hbm, data_hbm, adj_out, grad_out,
    lk, sto, act_in, adj, pump, cells, data, local, kpad, hpad, zpad, lpad, klog, krim, faces, slopes, rim_coef, self_t, diag, inv, rhs,
    p_now, g0, g1, y1, z0r, g0r, z1r, g1r, hrim, msg, inbox, gpart, pair_in, gsum, piece_in, gfull,
    far_in, send, recv,
):
    me = lax.axis_index("slab")
    test = lax.axis_index("test")
    above, below = lax.rem(me + 1, SLABS), lax.rem(me + SLABS - 1, SLABS)
    chip, core = test // 2, lax.rem(test, 2)
    sibling = test + 1 - 2 * core
    mates = [lax.rem(test + 2 * i, 8) for i in (1, 2, 3)]
    plane_at, deep = me // 4, lax.rem(me, 4)
    col, line = lax.rem(plane_at, 4), plane_at // 4
    z_part = [plane_at * 4 + lax.rem(deep + i, 4) for i in (1, 2, 3)]
    xy_part = [
        (lax.rem(line + j, 4) * 4 + lax.rem(col + i, 4)) * 4 + deep
        for j in range(4) for i in range(4) if i or j
    ]
    loads = [
        pltpu.make_async_copy(src, dst, local.at[n])
        for n, (src, dst) in enumerate((
            (pump_hbm, pump), (cells_hbm, cells), (data_hbm, data),
            (hd_hbm, hpad.at[:, pl.ds(PAD, ROWS)]), (lk_hbm, lk), (sto_hbm, sto), (act_hbm, act_in),
            (adj_hbm, adj),
        ))
    ]
    barrier = pltpu.get_barrier_semaphore()
    for other in [above, below] + z_part + xy_part:
        pl.semaphore_signal(barrier, inc=1, device_id={"slab": other}, device_id_type=MESH)
    for other in [sibling] + mates:
        pl.semaphore_signal(barrier, inc=1, device_id={"test": other}, device_id_type=MESH)
    for load in loads:
        load.start()
    copies = Copies(send, recv)
    pending = []

    def begin(src, dst, **where):
        copy = copies.start(src, dst, **where)
        pending.append(copy)
        return copy

    own = pl.ds(pl.multiple_of(core * HALF + chip * PIECE, PIECE), PIECE)
    own_half = pl.ds(pl.multiple_of(core * HALF, HALF), HALF)

    pl.semaphore_wait(barrier, 24)
    to_above = begin(lk_hbm.at[1, own], klog.at[0, own], slab=above)
    to_below = begin(lk_hbm.at[0, own], klog.at[1, own], slab=below)

    def send_heads(first, size):
        up, down = pl.ds(first, size), pl.ds(HALF + first, size)
        return [
            begin(hd_hbm.at[1, up], hrim.at[up], slab=above),
            begin(hd_hbm.at[0, down], hrim.at[down], slab=below),
        ]

    head_copies = send_heads(0, EARLY)

    low_pad = jnp.zeros((2, PAD, LANES), jnp.float32)
    for ref, fill in ((kpad, 1.0), (hpad, 0.0), (zpad, 0.0), (lpad, 0.0)):
        ref[:, pl.ds(0, PAD), :] = low_pad + fill
        ref[:, pl.ds(PAD + ROWS, PAD), :] = low_pad + fill

    for load in loads:
        load.wait()
    offset = me * (2 * ROWS)
    eye = lax.broadcasted_iota(jnp.int32, (NOBS, NOBS), 0) == lax.broadcasted_iota(jnp.int32, (NOBS, NOBS), 1)

    def upright(row):
        return jnp.sum(jnp.where(eye, row, 0.0), axis=1, keepdims=True)

    row_of = cells[...] // LANES
    lane_of = upright((cells[...] - row_of * LANES).astype(jnp.float32))
    row_of = row_of - offset
    cell_row = upright(row_of.astype(jnp.float32))
    lane_index = lax.broadcasted_iota(jnp.int32, (NOBS, LANES), 1).astype(jnp.float32)
    picked = jnp.zeros((NOBS, LANES), jnp.float32)
    for x in range(2):
        index = lax.broadcasted_iota(jnp.int32, (NOBS, ROWS), 1) + x * ROWS
        picked = picked + jnp.dot(
            (index.astype(jnp.float32) == cell_row).astype(jnp.float32), hpad[x, pl.ds(PAD, ROWS), :],
            precision=lax.Precision.HIGHEST, preferred_element_type=jnp.float32,
        )
    values = jnp.where(lane_index == lane_of, picked - upright(data[...]), 0.0)
    for x in range(2):
        index = lax.broadcasted_iota(jnp.int32, (ROWS, NOBS), 0) + x * ROWS
        rhs[x] = jnp.dot(
            (index == row_of).astype(jnp.float32), values,
            precision=lax.Precision.HIGHEST, preferred_element_type=jnp.float32,
        )

    well_at = pump[0] - offset * LANES
    shape = (2, BLOCK, LANES)
    lane_no = lax.broadcasted_iota(jnp.int32, shape, 2)
    row_no = lax.broadcasted_iota(jnp.int32, shape, 1)
    cell_no = lax.broadcasted_iota(jnp.int32, shape, 0) * (ROWS * LANES) + row_no * LANES + lane_no

    def prepare(i, carry):
        at = pl.multiple_of(i * BLOCK, BLOCK)
        here = rows_at(at)
        kpad[:, rows_at(pl.multiple_of(PAD + at, 8)), :] = jnp.exp(lk[:, here, :])
        return carry

    lax.fori_loop(0, ROWS // BLOCK, prepare, 0)

    def local_terms(i, carry):
        at = pl.multiple_of(i * BLOCK, BLOCK)
        here = rows_at(at)
        k = kpad[:, rows_at(pl.multiple_of(PAD + at, 8)), :]
        total = jnp.zeros(shape, jnp.float32)
        sides = (
            (kpad[:, rows_at(PAD - 1 + at), :], row_no + at > 0),
            (kpad[:, rows_at(PAD + 1 + at), :], row_no + at < ROWS - 1),
            (pltpu.roll(k, 1, 2), lane_no > 0),
            (pltpu.roll(k, LANES - 1, 2), lane_no < LANES - 1),
        )
        for n, (other, inside) in enumerate(sides):
            both = k + other
            face = jnp.where(inside, 2.0 * k * other / both, 0.0)
            faces[n, :, here, :] = face
            slopes[n, :, here, :] = face * other / both
            total = total + face
        both = k[0] + k[1]
        face = 2.0 * k[0] * k[1] / both
        rim_coef[0, here, :] = face
        rim_coef[1, here, :] = face * k[1] / both
        rim_coef[2, here, :] = face * k[0] / both
        well = jnp.where(cell_no + at * LANES == well_at, WELL_TERM, 0.0)
        self_here = sto[:, here, :] + well
        self_t[:, here, :] = self_here
        diag[:, here, :] = self_here + total + face[None]
        active = act_in[:, here, :].astype(jnp.float32)
        rhs[:, here, :] = active * (sto[:, here, :] * adj[:, here, :] + rhs[:, here, :])
        return carry

    lax.fori_loop(0, ROWS // BLOCK, local_terms, 0)

    def gather(ref, arrived):
        for copy in arrived:
            copy.wait_recv()
        around = [begin(ref.at[:, own], ref.at[:, own], test=mate) for mate in mates]
        for copy in around:
            copy.wait_recv()
        begin(ref.at[:, own_half], ref.at[:, own_half], test=sibling).wait_recv()

    gather(klog, [to_above, to_below])

    low_edge = jnp.where(me > 0, 1.0, 0.0)
    high_edge = jnp.where(me < SLABS - 1, 1.0, 0.0)

    def rim_terms(i, carry):
        at = pl.multiple_of(i * BLOCK, BLOCK)
        here = rows_at(at)
        k = kpad[:, rows_at(pl.multiple_of(PAD + at, 8)), :]
        other = jnp.exp(klog[:, here, :])
        krim[:, here, :] = other
        both = k + other
        face = 2.0 * k * other / both
        low = face[0] * low_edge
        high = face[1] * high_edge
        rim_coef[3, here, :] = low
        rim_coef[4, here, :] = high
        rim_coef[5, here, :] = low * other[0] / both[0]
        rim_coef[6, here, :] = high * other[1] / both[1]
        rim_coef[7, here, :] = low * k[0] / both[0]
        rim_coef[8, here, :] = high * k[1] / both[1]
        active = act_in[:, here, :].astype(jnp.float32)
        fixed = 1.0 - active
        d0 = active[0] * (diag[0, here, :] + low) + fixed[0]
        d1 = active[1] * (diag[1, here, :] + high) + fixed[1]
        diag[0, here, :] = d0
        diag[1, here, :] = d1
        inv[0, here, :] = 1.0 / d0
        inv[1, here, :] = 1.0 / d1
        there = rows_at(pl.multiple_of(PAD + at, 8))
        z0 = rhs[0, here, :] / d0
        z1 = rhs[1, here, :] / d1
        zpad[0, there, :] = z0
        zpad[1, there, :] = z1
        p_now[0, here, :] = z0
        p_now[1, here, :] = z1
        return carry

    def send_rims(ref, pad, rims, chunk):
        src = pl.ds(pad + chunk * CHUNK, CHUNK)
        dst = pl.ds(chunk * CHUNK, CHUNK)
        return [
            begin(ref.at[1, src], rims.at[0, dst], slab=above),
            begin(ref.at[0, src], rims.at[1, dst], slab=below),
        ]

    per_chunk = CHUNK // BLOCK
    z_copies = {}
    for chunk in ORDER:
        lax.fori_loop(chunk * per_chunk, (chunk + 1) * per_chunk, rim_terms, 0)
        z_copies[chunk] = send_rims(zpad, PAD, z0r, chunk)

    def image_of(at, rim_low, rim_high):
        here = rows_at(at)
        there = rows_at(pl.multiple_of(PAD + at, 8))
        z = zpad[:, there, :]
        flux = faces[0, :, here, :] * (z - zpad[:, rows_at(PAD - 1 + at), :])
        flux = flux + faces[1, :, here, :] * (z - zpad[:, rows_at(PAD + 1 + at), :])
        flux = flux + faces[2, :, here, :] * (z - pltpu.roll(z, 1, 2))
        flux = flux + faces[3, :, here, :] * (z - pltpu.roll(z, LANES - 1, 2))
        across = rim_coef[0, here, :] * (z[0] - z[1])
        low = across + rim_coef[3, here, :] * (z[0] - rim_low)
        high = rim_coef[4, here, :] * (z[1] - rim_high) - across
        active = act_in[:, here, :].astype(jnp.float32)
        body = self_t[:, here, :] * z + flux
        image0 = active[0] * (body[0] + low) + (1.0 - active[0]) * z[0]
        image1 = active[1] * (body[1] + high) + (1.0 - active[1]) * z[1]
        return z, image0, image1

    zero = jnp.zeros((BLOCK, LANES), jnp.float32)

    def inner_terms(sums, z, image0, image1, d):
        rz = sums[0] + z[0] * z[0] * d[0] + z[1] * z[1] * d[1]
        pw = sums[1] + z[0] * image0 + z[1] * image1
        return rz, pw

    def all_sum(which, sums, between):
        first = jnp.concatenate([jnp.sum(s, axis=0, keepdims=True) for s in sums], axis=0)
        n = 0
        for stage in (z_part, xy_part):
            msg[which, n] = first
            batch = [
                begin(msg.at[which, n], inbox.at[which, n + i], slab=other)
                for i, other in enumerate(stage)
            ]
            if n == 0:
                between()
            for copy in batch:
                copy.wait_recv()
            for i in range(len(stage)):
                first = first + inbox[which, n + i]
            n += len(stage)
        total = jnp.sum(first, axis=1, keepdims=True)
        total = jnp.broadcast_to(total, (2, LANES))
        return total[0:1], total[1:2]

    def first_image(i, sums):
        at = pl.multiple_of(i * BLOCK, BLOCK)
        here = rows_at(at)
        z, image0, image1 = image_of(at, z0r[0, here, :], z0r[1, here, :])
        g0[0, here, :] = image0 * inv[0, here, :]
        g0[1, here, :] = image1 * inv[1, here, :]
        return inner_terms(sums, z, image0, image1, diag[:, here, :])

    sums = (zero, zero)
    g0_copies = {}

    def send_g0(chunks):
        for chunk in chunks:
            g0_copies[chunk] = send_rims(g0, 0, g0r, chunk)

    for n, chunk in enumerate(ORDER):
        for copy in z_copies[chunk]:
            copy.wait_recv()
        sums = lax.fori_loop(chunk * per_chunk, (chunk + 1) * per_chunk, first_image, sums)
        if n < 2:
            send_g0([chunk])
    done = [copy for chunk in ORDER for copy in z_copies[chunk]]
    rz0, pw0 = all_sum(0, sums, lambda: send_g0(ORDER[2:]))
    for copy in done:
        copy.wait_send()
    pending[:] = [copy for copy in pending if all(copy is not other for other in done)]
    alpha0 = rz0 / pw0

    def step_one(i, carry):
        at = pl.multiple_of(i * BLOCK, BLOCK)
        here = rows_at(at)
        zpad[:, rows_at(pl.multiple_of(PAD + at, 8)), :] = p_now[:, here, :] - alpha0 * g0[:, here, :]
        return carry

    lax.fori_loop(0, ROWS // BLOCK, step_one, 0)

    def second_image(i, sums):
        at = pl.multiple_of(i * BLOCK, BLOCK)
        here = rows_at(at)
        rim = z0r[:, here, :] - alpha0 * g0r[:, here, :]
        z1r[:, here, :] = rim
        z, image0, image1 = image_of(at, rim[0], rim[1])
        g1[0, here, :] = image0 * inv[0, here, :]
        g1[1, here, :] = image1 * inv[1, here, :]
        return inner_terms(sums, z, image0, image1, diag[:, here, :])

    sums = (zero, zero)
    g1_copies = {}

    def send_g1(chunks):
        for chunk in chunks:
            part = pl.ds(chunk * CHUNK, CHUNK)
            if chunk < CHUNKS // 2:
                g1_copies[chunk] = begin(g1.at[1, part], g1r.at[part], slab=above)
            else:
                g1_copies[chunk] = begin(g1.at[0, part], g1r.at[part], slab=below)

    for n, chunk in enumerate(ORDER):
        for copy in g0_copies[chunk]:
            copy.wait_recv()
        sums = lax.fori_loop(chunk * per_chunk, (chunk + 1) * per_chunk, second_image, sums)
        if n < 2:
            send_g1([chunk])
    rz1, delta1 = all_sum(1, sums, lambda: send_g1(ORDER[2:]))
    beta0 = rz1 / rz0
    alpha1 = rz1 / (delta1 - beta0 * rz1 / alpha0)

    def step_two(i, carry):
        at = pl.multiple_of(i * BLOCK, BLOCK)
        here = rows_at(at)
        there = rows_at(pl.multiple_of(PAD + at, 8))
        z = zpad[:, there, :]
        p0 = p_now[:, here, :]
        p1 = z + beta0 * p0
        lpad[:, there, :] = alpha0 * p0 + alpha1 * p1
        p_now[:, here, :] = p1
        zpad[:, there, :] = z - alpha1 * (g1[:, here, :] + beta0 * g0[:, here, :])
        return carry

    lax.fori_loop(0, ROWS // BLOCK, step_two, 0)

    def energy(side, i, sums):
        at = pl.multiple_of(i * BLOCK, BLOCK)
        here = rows_at(at)
        z = zpad[:, rows_at(pl.multiple_of(PAD + at, 8)), :]
        z0 = z0r[side, here, :]
        z1 = z1r[side, here, :]
        p1 = z1 + beta0 * z0
        rim = z1 - alpha1 * (g1r[here, :] + beta0 * g0r[side, here, :])
        y1[0, here, :] = rim
        y1[1, here, :] = p1
        z1r[side, here, :] = alpha0 * z0 + alpha1 * p1
        up = z - zpad[:, rows_at(PAD + 1 + at), :]
        right = z - pltpu.roll(z, LANES - 1, 2)
        across = z[0] - z[1]
        over = z[side] - rim
        square = faces[1, :, here, :] * up * up + faces[3, :, here, :] * right * right
        square = square + self_t[:, here, :] * z * z
        active = act_in[:, here, :].astype(jnp.float32)
        fixed = (1.0 - active) * z * z
        square = square + fixed
        pw = sums[1] + square[0] + square[1] + rim_coef[0, here, :] * across * across
        pw = pw + rim_coef[3 + side, here, :] * over * over
        d = diag[:, here, :]
        rz = sums[0] + z[0] * z[0] * d[0] + z[1] * z[1] * d[1]
        return rz, pw

    sums = (zero, zero)
    for chunk in ORDER:
        g1_copies[chunk].wait_recv()
        side = 0 if chunk < CHUNKS // 2 else 1
        sums = lax.fori_loop(
            chunk * per_chunk, (chunk + 1) * per_chunk, functools.partial(energy, side), sums
        )
    rz2, delta2 = all_sum(2, sums, lambda: head_copies.extend(send_heads(EARLY, HALF - EARLY)))
    beta1 = rz2 / rz1
    alpha2 = rz2 / (delta2 - beta1 * rz2 / alpha1)

    def last_step(i, carry):
        at = pl.multiple_of(i * BLOCK, BLOCK)
        here = rows_at(at)
        there = rows_at(pl.multiple_of(PAD + at, 8))
        new = lpad[:, there, :] + alpha2 * (zpad[:, there, :] + beta1 * p_now[:, here, :])
        lpad[:, there, :] = new
        adj[:, here, :] = -new
        return carry

    lax.fori_loop(0, ROWS // BLOCK, last_step, 0)

    store = pltpu.make_async_copy(adj, adj_out, local.at[0])
    store.start()
    for copy in head_copies:
        copy.wait_recv()

    def gradient(side, i, carry):
        at = pl.multiple_of(i * BLOCK, BLOCK)
        here = rows_at(at)
        there = rows_at(pl.multiple_of(PAD + at, 8))
        lam = lpad[:, there, :]
        head = hpad[:, there, :]
        lower, upper = rows_at(PAD - 1 + at), rows_at(PAD + 1 + at)
        total = slopes[0, :, here, :] * (lam - lpad[:, lower, :]) * (head - hpad[:, lower, :])
        total = total + slopes[1, :, here, :] * (lam - lpad[:, upper, :]) * (head - hpad[:, upper, :])
        for n, turn in ((2, 1), (3, LANES - 1)):
            total = total + slopes[n, :, here, :] * (lam - pltpu.roll(lam, turn, 2)) * (
                head - pltpu.roll(head, turn, 2)
            )
        across = (lam[0] - lam[1]) * (head[0] - head[1])
        rim = z1r[side, here, :] + alpha2 * (y1[0, here, :] + beta1 * y1[1, here, :])
        over = (lam[side] - rim) * (head[side] - hrim[here, :])
        total0 = total[0] + rim_coef[1, here, :] * across
        total1 = total[1] + rim_coef[2, here, :] * across
        if side == 0:
            total0 = total0 + rim_coef[5, here, :] * over
        else:
            total1 = total1 + rim_coef[6, here, :] * over
        gpart[0, here, :] = total0
        gpart[1, here, :] = total1
        gpart[2, here, :] = rim_coef[7 + side, here, :] * over
        return carry

    blocks = HALF // BLOCK
    lax.fori_loop(0, blocks, functools.partial(gradient, 0), 0)
    lax.fori_loop(blocks, 2 * blocks, functools.partial(gradient, 1), 0)

    other_half = pl.ds(pl.multiple_of((1 - core) * HALF, HALF), HALF)
    quarter = pl.ds(pl.multiple_of(chip * PIECE, PIECE), PIECE)
    parts = (pl.ds(2, 1), pl.ds(0, 2))
    pairs = [begin(gpart.at[part, other_half], pair_in.at[part], test=sibling) for part in parts]
    spread = []
    for part, pair in zip(parts, pairs):
        pair.wait_recv()
        gsum[part] = gpart[part, own_half, :] + pair_in[part]
        spread.append([
            begin(
                gsum.at[part, pl.ds(pl.multiple_of(lax.rem(chip + i + 1, 4) * PIECE, PIECE), PIECE)],
                piece_in.at[i, part], test=mate,
            )
            for i, mate in enumerate(mates)
        ])

    def summed(part):
        return gsum[part, quarter, :] + piece_in[0, part] + piece_in[1, part] + piece_in[2, part]

    for copy in spread[0]:
        copy.wait_recv()
    far_in[pl.ds(0, 1)] = summed(parts[0])
    toward = jnp.where(core == 0, below, above)
    far = begin(far_in.at[0], far_in.at[1], slab=toward)
    for copy in spread[1]:
        copy.wait_recv()
    gfull[:, own, :] = summed(parts[1])
    around = [begin(gfull.at[core, own], gfull.at[core, own], test=mate) for mate in mates]
    far.wait_recv()
    gfull[1 - core, own, :] = gfull[1 - core, own, :] + far_in[1]
    rest = [begin(gfull.at[1 - core, own], gfull.at[1 - core, own], test=mate) for mate in mates]
    for copy in around:
        copy.wait_recv()
    swap = begin(gfull.at[core, own_half], gfull.at[core, own_half], test=sibling)
    for copy in rest:
        copy.wait_recv()
    last = begin(gfull.at[1 - core, own_half], gfull.at[1 - core, own_half], test=sibling)
    swap.wait_recv()
    last.wait_recv()
    result = pltpu.make_async_copy(gfull, grad_out, local.at[1])
    result.start()
    store.wait()
    result.wait()
    for copy in pending:
        copy.wait_send()


def on_device(
    log_conductivity, storage, active_mask, heads, adjoint_next, pump_cells, obs_cells, obs_data
):
    full = (2, ROWS, LANES)
    one = (ROWS, LANES)
    padded = (2, ROWS + 2 * PAD, LANES)
    f32 = lambda *s: pltpu.VMEM(s, jnp.float32)
    anywhere = pl.BlockSpec(memory_space=pl.ANY)
    adjoint, gradient = pl.pallas_call(
        kernel,
        out_shape=[jax.ShapeDtypeStruct(full, jnp.float32)] * 2,
        in_specs=[anywhere] * 8,
        out_specs=[anywhere] * 2,
        scratch_shapes=[
            f32(*full), f32(*full), pltpu.VMEM(full, jnp.int32), f32(*full),
            pltpu.SMEM((1,), jnp.int32), pltpu.VMEM((1, NOBS), jnp.int32), f32(1, NOBS),
            pltpu.SemaphoreType.DMA((8,)),
            f32(*padded), f32(*padded), f32(*padded), f32(*padded),
            f32(*full), f32(*full), f32(4, *full), f32(4, *full), f32(9, *one),
            f32(*full), f32(*full), f32(*full), f32(*full),
            f32(*full), f32(*full), f32(*full), f32(*full),
            f32(*full), f32(*full), f32(*full), f32(*one), f32(*one),
            f32(3, 18, 2, LANES), f32(3, 18, 2, LANES),
            f32(3, *one), f32(3, HALF, LANES), f32(3, HALF, LANES), f32(3, 3, PIECE, LANES), f32(*full),
            f32(2, PIECE, LANES),
            pltpu.SemaphoreType.DMA((N_COPIES,)),
            pltpu.SemaphoreType.DMA((N_COPIES,)),
        ],
        compiler_params=pltpu.CompilerParams(
            collective_id=0, has_side_effects=True, vmem_limit_bytes=56 << 20
        ),
    )(
        log_conductivity, storage, active_mask, heads[0], adjoint_next[0], pump_cells,
        obs_cells.reshape(1, NOBS), obs_data,
    )
    return (-adjoint)[None], -gradient


def solution(mesh):
    return jax.shard_map(
        on_device,
        mesh=mesh,
        in_specs=(
            P("slab", None, None),
            P("slab", None, None),
            P("slab", None, None),
            P("test", "slab", None, None),
            P("test", "slab", None, None),
            P("test"),
            P(),
            P("test", None),
        ),
        out_specs=(P("test", "slab", None, None), P("slab", None, None)),
        check_vma=False,
    )
```

```python
import functools

import jax
import jax.numpy as jnp
from jax import lax
from jax.experimental import pallas as pl
from jax.experimental.pallas import tpu as pltpu
from jax.sharding import PartitionSpec as P

MESH = pl.DeviceIdType.MESH
WELL_TERM = 4.0
SLABS = 64
ROWS = 512
LANES = 128
NOBS = 64
PAD = 8
BLOCK = 16
CHUNK = 128
CHUNKS = ROWS // CHUNK
HALF = ROWS // 2
PIECE = 64


class Copies:
    def __init__(self, send, recv):
        self.send, self.recv, self.count = send, recv, 0

    def start(self, src, dst, **where):
        copy = pltpu.make_async_remote_copy(
            src_ref=src,
            dst_ref=dst,
            send_sem=self.send.at[self.count],
            recv_sem=self.recv.at[self.count],
            device_id=where,
            device_id_type=MESH,
        )
        self.count += 1
        copy.start()
        return copy


ORDER = (0, 2, 1, 3)
AHEAD = 2
STAGE = 0
STEP_MIN = 0.5
STEP_MAX = 3400.0
N_COPIES = 2 + 4 + 2 + 2 * CHUNKS + 2 * CHUNKS + CHUNKS + 2 * 18 + 2 + 6 + 1 + 8


def rows_at(start, size=BLOCK):
    return pl.ds(start, size)


def kernel(
    lk_hbm, sto_hbm, act_hbm, hd_hbm, adj_hbm, pump_hbm, cells_hbm, data_hbm, adj_out, grad_out,
    lk, sto, act_in, adj, pump, cells, data, local, kpad, hpad, zpad, lpad, klog, krim, faces, slopes, rim_coef, self_t, diag, inv, rhs,
    vpad, tpad, z1, v2, z0r, v1r, z1r, t1r, v2r, hrim, msg, inbox, gpart, pair_in, gsum, piece_in, gfull,
    far_in, send, recv,
):
    me = lax.axis_index("slab")
    test = lax.axis_index("test")
    above, below = lax.rem(me + 1, SLABS), lax.rem(me + SLABS - 1, SLABS)
    chip, core = test // 2, lax.rem(test, 2)
    sibling = test + 1 - 2 * core
    mates = [lax.rem(test + 2 * i, 8) for i in (1, 2, 3)]
    plane_at, deep = me // 4, lax.rem(me, 4)
    col, line = lax.rem(plane_at, 4), plane_at // 4
    z_part = [plane_at * 4 + lax.rem(deep + i, 4) for i in (1, 2, 3)]
    xy_part = [
        (lax.rem(line + j, 4) * 4 + lax.rem(col + i, 4)) * 4 + deep
        for j in range(4) for i in range(4) if i or j
    ]
    loads = [
        pltpu.make_async_copy(src, dst, local.at[n])
        for n, (src, dst) in enumerate((
            (pump_hbm, pump), (cells_hbm, cells), (data_hbm, data),
            (hd_hbm, hpad.at[:, pl.ds(PAD, ROWS)]), (lk_hbm, lk), (sto_hbm, sto), (act_hbm, act_in),
            (adj_hbm, adj),
        ))
    ]
    barrier = pltpu.get_barrier_semaphore()
    for other in [above, below] + z_part + xy_part:
        pl.semaphore_signal(barrier, inc=1, device_id={"slab": other}, device_id_type=MESH)
    for other in [sibling] + mates:
        pl.semaphore_signal(barrier, inc=1, device_id={"test": other}, device_id_type=MESH)
    for load in loads:
        load.start()
    copies = Copies(send, recv)
    pending = []

    def begin(src, dst, **where):
        copy = copies.start(src, dst, **where)
        pending.append(copy)
        return copy

    own = pl.ds(pl.multiple_of(core * HALF + chip * PIECE, PIECE), PIECE)
    own_half = pl.ds(pl.multiple_of(core * HALF, HALF), HALF)

    pl.semaphore_wait(barrier, 24)
    to_above = begin(lk_hbm.at[1, own], klog.at[0, own], slab=above)
    to_below = begin(lk_hbm.at[0, own], klog.at[1, own], slab=below)

    def send_heads(first, size):
        up, down = pl.ds(first, size), pl.ds(HALF + first, size)
        return [
            begin(hd_hbm.at[1, up], hrim.at[up], slab=above),
            begin(hd_hbm.at[0, down], hrim.at[down], slab=below),
        ]


    low_pad = jnp.zeros((2, PAD, LANES), jnp.float32)
    for ref, fill in ((kpad, 1.0), (hpad, 0.0), (zpad, 0.0), (lpad, 0.0), (vpad, 0.0), (tpad, 0.0)):
        ref[:, pl.ds(0, PAD), :] = low_pad + fill
        ref[:, pl.ds(PAD + ROWS, PAD), :] = low_pad + fill

    for load in loads:
        load.wait()
    offset = me * (2 * ROWS)
    eye = lax.broadcasted_iota(jnp.int32, (NOBS, NOBS), 0) == lax.broadcasted_iota(jnp.int32, (NOBS, NOBS), 1)

    def upright(row):
        return jnp.sum(jnp.where(eye, row, 0.0), axis=1, keepdims=True)

    row_of = cells[...] // LANES
    lane_of = upright((cells[...] - row_of * LANES).astype(jnp.float32))
    row_of = row_of - offset
    cell_row = upright(row_of.astype(jnp.float32))
    lane_index = lax.broadcasted_iota(jnp.int32, (NOBS, LANES), 1).astype(jnp.float32)
    picked = jnp.zeros((NOBS, LANES), jnp.float32)
    for x in range(2):
        index = lax.broadcasted_iota(jnp.int32, (NOBS, ROWS), 1) + x * ROWS
        picked = picked + jnp.dot(
            (index.astype(jnp.float32) == cell_row).astype(jnp.float32), hpad[x, pl.ds(PAD, ROWS), :],
            precision=lax.Precision.HIGHEST, preferred_element_type=jnp.float32,
        )
    values = jnp.where(lane_index == lane_of, picked - upright(data[...]), 0.0)
    for x in range(2):
        index = lax.broadcasted_iota(jnp.int32, (ROWS, NOBS), 0) + x * ROWS
        rhs[x] = jnp.dot(
            (index == row_of).astype(jnp.float32), values,
            precision=lax.Precision.HIGHEST, preferred_element_type=jnp.float32,
        )

    well_at = pump[0] - offset * LANES
    shape = (2, BLOCK, LANES)
    lane_no = lax.broadcasted_iota(jnp.int32, shape, 2)
    row_no = lax.broadcasted_iota(jnp.int32, shape, 1)
    cell_no = lax.broadcasted_iota(jnp.int32, shape, 0) * (ROWS * LANES) + row_no * LANES + lane_no

    def prepare(i, carry):
        at = pl.multiple_of(i * BLOCK, BLOCK)
        here = rows_at(at)
        kpad[:, rows_at(pl.multiple_of(PAD + at, 8)), :] = jnp.exp(lk[:, here, :])
        return carry

    lax.fori_loop(0, ROWS // BLOCK, prepare, 0)

    def local_terms(i, carry):
        at = pl.multiple_of(i * BLOCK, BLOCK)
        here = rows_at(at)
        k = kpad[:, rows_at(pl.multiple_of(PAD + at, 8)), :]
        total = jnp.zeros(shape, jnp.float32)
        sides = (
            (kpad[:, rows_at(PAD - 1 + at), :], row_no + at > 0),
            (kpad[:, rows_at(PAD + 1 + at), :], row_no + at < ROWS - 1),
            (pltpu.roll(k, 1, 2), lane_no > 0),
            (pltpu.roll(k, LANES - 1, 2), lane_no < LANES - 1),
        )
        for n, (other, inside) in enumerate(sides):
            both = k + other
            face = jnp.where(inside, 2.0 * k * other / both, 0.0)
            faces[n, :, here, :] = face
            slopes[n, :, here, :] = face * other / both
            total = total + face
        both = k[0] + k[1]
        face = 2.0 * k[0] * k[1] / both
        rim_coef[0, here, :] = face
        rim_coef[1, here, :] = face * k[1] / both
        rim_coef[2, here, :] = face * k[0] / both
        well = jnp.where(cell_no + at * LANES == well_at, WELL_TERM, 0.0)
        self_here = sto[:, here, :] + well
        self_t[:, here, :] = self_here
        diag[:, here, :] = self_here + total + face[None]
        active = act_in[:, here, :].astype(jnp.float32)
        rhs[:, here, :] = active * (sto[:, here, :] * adj[:, here, :] + rhs[:, here, :])
        return carry

    lax.fori_loop(0, ROWS // BLOCK, local_terms, 0)

    def gather(ref, arrived):
        for copy in arrived:
            copy.wait_recv()
        around = [begin(ref.at[:, own], ref.at[:, own], test=mate) for mate in mates]
        for copy in around:
            copy.wait_recv()
        begin(ref.at[:, own_half], ref.at[:, own_half], test=sibling).wait_recv()

    gather(klog, [to_above, to_below])

    low_edge = jnp.where(me > 0, 1.0, 0.0)
    high_edge = jnp.where(me < SLABS - 1, 1.0, 0.0)

    def rim_terms(i, carry):
        at = pl.multiple_of(i * BLOCK, BLOCK)
        here = rows_at(at)
        k = kpad[:, rows_at(pl.multiple_of(PAD + at, 8)), :]
        other = jnp.exp(klog[:, here, :])
        krim[:, here, :] = other
        both = k + other
        face = 2.0 * k * other / both
        low = face[0] * low_edge
        high = face[1] * high_edge
        rim_coef[3, here, :] = low
        rim_coef[4, here, :] = high
        rim_coef[5, here, :] = low * other[0] / both[0]
        rim_coef[6, here, :] = high * other[1] / both[1]
        rim_coef[7, here, :] = low * k[0] / both[0]
        rim_coef[8, here, :] = high * k[1] / both[1]
        active = act_in[:, here, :].astype(jnp.float32)
        fixed = 1.0 - active
        d0 = active[0] * (diag[0, here, :] + low) + fixed[0]
        d1 = active[1] * (diag[1, here, :] + high) + fixed[1]
        diag[0, here, :] = d0
        diag[1, here, :] = d1
        inv[0, here, :] = 1.0 / d0
        inv[1, here, :] = 1.0 / d1
        there = rows_at(pl.multiple_of(PAD + at, 8))
        z0 = rhs[0, here, :] / d0
        z1 = rhs[1, here, :] / d1
        zpad[0, there, :] = z0
        zpad[1, there, :] = z1
        return carry

    def send_rims(ref, pad, rims, chunk):
        src = pl.ds(pad + chunk * CHUNK, CHUNK)
        dst = pl.ds(chunk * CHUNK, CHUNK)
        return [
            begin(ref.at[1, src], rims.at[0, dst], slab=above),
            begin(ref.at[0, src], rims.at[1, dst], slab=below),
        ]

    per_chunk = CHUNK // BLOCK
    z_copies = {}
    for chunk in ORDER:
        lax.fori_loop(chunk * per_chunk, (chunk + 1) * per_chunk, rim_terms, 0)
        z_copies[chunk] = send_rims(zpad, PAD, z0r, chunk)

    def image_of(ref, at, rim_low, rim_high):
        here = rows_at(at)
        z = ref[:, rows_at(pl.multiple_of(PAD + at, 8)), :]
        flux = faces[0, :, here, :] * (z - ref[:, rows_at(PAD - 1 + at), :])
        flux = flux + faces[1, :, here, :] * (z - ref[:, rows_at(PAD + 1 + at), :])
        flux = flux + faces[2, :, here, :] * (z - pltpu.roll(z, 1, 2))
        flux = flux + faces[3, :, here, :] * (z - pltpu.roll(z, LANES - 1, 2))
        across = rim_coef[0, here, :] * (z[0] - z[1])
        low = across + rim_coef[3, here, :] * (z[0] - rim_low)
        high = rim_coef[4, here, :] * (z[1] - rim_high) - across
        active = act_in[:, here, :].astype(jnp.float32)
        body = self_t[:, here, :] * z + flux
        image0 = active[0] * (body[0] + low) + (1.0 - active[0]) * z[0]
        image1 = active[1] * (body[1] + high) + (1.0 - active[1]) * z[1]
        return z, image0, image1

    zero = jnp.zeros((BLOCK, LANES), jnp.float32)

    class Sum:
        def __init__(self, which, sums):
            rows = [jnp.sum(s, axis=0, keepdims=True) for s in sums]
            rows = rows + [jnp.zeros((1, LANES), jnp.float32)] * (8 - len(rows))
            self.which, self.n, self.value = which, 0, jnp.concatenate(rows, axis=0)

        def start(self, stage):
            msg[self.which, self.n] = self.value
            self.batch = [
                begin(msg.at[self.which, self.n], inbox.at[self.which, self.n + i], slab=other)
                for i, other in enumerate(stage)
            ]

        def finish(self):
            for copy in self.batch:
                copy.wait_recv()
            for i in range(len(self.batch)):
                self.value = self.value + inbox[self.which, self.n + i]
            self.n += len(self.batch)

        def total(self):
            total = jnp.broadcast_to(jnp.sum(self.value, axis=1, keepdims=True), (8, LANES))
            return [total[i:i + 1] for i in range(8)]

    def first_image(i, sums):
        at = pl.multiple_of(i * BLOCK, BLOCK)
        here = rows_at(at)
        there = rows_at(pl.multiple_of(PAD + at, 8))
        z, image0, image1 = image_of(zpad, at, z0r[0, here, :], z0r[1, here, :])
        vpad[0, there, :] = image0 * inv[0, here, :]
        vpad[1, there, :] = image1 * inv[1, here, :]
        d = diag[:, here, :]
        rz = sums[0] + z[0] * z[0] * d[0] + z[1] * z[1] * d[1]
        return rz, sums[1] + z[0] * image0 + z[1] * image1

    sums = (zero, zero)
    v1_copies = {}

    def send_v1(chunks):
        for chunk in chunks:
            v1_copies[chunk] = send_rims(vpad, PAD, v1r, chunk)

    for n, chunk in enumerate(ORDER):
        for copy in z_copies[chunk]:
            copy.wait_recv()
        sums = lax.fori_loop(chunk * per_chunk, (chunk + 1) * per_chunk, first_image, sums)
        if n < AHEAD:
            send_v1([chunk])
    first_sum = Sum(0, sums)
    first_sum.start(z_part)
    send_v1(ORDER[AHEAD:])

    def second_image(i, carry):
        at = pl.multiple_of(i * BLOCK, BLOCK)
        here = rows_at(at)
        _, image0, image1 = image_of(vpad, at, v1r[0, here, :], v1r[1, here, :])
        v2[0, here, :] = image0 * inv[0, here, :]
        v2[1, here, :] = image1 * inv[1, here, :]
        return carry

    v2_copies = {}
    for n, chunk in enumerate(ORDER):
        for copy in v1_copies[chunk]:
            copy.wait_recv()
        lax.fori_loop(chunk * per_chunk, (chunk + 1) * per_chunk, second_image, 0)
        part = pl.ds(chunk * CHUNK, CHUNK)
        if chunk < CHUNKS // 2:
            v2_copies[chunk] = begin(v2.at[1, part], v2r.at[part], slab=above)
        else:
            v2_copies[chunk] = begin(v2.at[0, part], v2r.at[part], slab=below)
        if n == STAGE:
            first_sum.finish()
            first_sum.start(xy_part)
    first_sum.finish()
    rz0, pw0 = first_sum.total()[:2]
    alpha0 = jnp.clip(rz0 / pw0, STEP_MIN, STEP_MAX)

    def step_one(i, sums):
        at = pl.multiple_of(i * BLOCK, BLOCK)
        here = rows_at(at)
        there = rows_at(pl.multiple_of(PAD + at, 8))
        v_one = vpad[:, there, :]
        v_two = v2[:, here, :]
        z_new = zpad[:, there, :] - alpha0 * v_one
        t_new = v_one - alpha0 * v_two
        z1[:, here, :] = z_new
        tpad[:, there, :] = t_new
        d = diag[:, here, :]
        z_d, t_d, v_d = z_new * d, t_new * d, v_one * d
        terms = (
            z_d * z_new, z_d * t_new, t_d * t_new, t_d * v_one, v_d * v_one, t_d * v_two, v_d * v_two,
        )
        return tuple(s + term[0] + term[1] for s, term in zip(sums, terms))

    sums = lax.fori_loop(0, ROWS // BLOCK, step_one, (zero,) * 7)

    def energy(side, i, total):
        at = pl.multiple_of(i * BLOCK, BLOCK)
        here = rows_at(at)
        t = tpad[:, rows_at(pl.multiple_of(PAD + at, 8)), :]
        v_rim = v1r[side, here, :]
        rim = v_rim - alpha0 * v2r[here, :]
        t1r[here, :] = rim
        z1r[here, :] = z0r[side, here, :] - alpha0 * v_rim
        up = t - tpad[:, rows_at(PAD + 1 + at), :]
        right = t - pltpu.roll(t, LANES - 1, 2)
        across = t[0] - t[1]
        over = t[side] - rim
        square = faces[1, :, here, :] * up * up + faces[3, :, here, :] * right * right
        square = square + self_t[:, here, :] * t * t
        active = act_in[:, here, :].astype(jnp.float32)
        square = square + (1.0 - active) * t * t
        total = total + square[0] + square[1] + rim_coef[0, here, :] * across * across
        return total + rim_coef[3 + side, here, :] * over * over

    tt_energy = zero
    for chunk in ORDER:
        v2_copies[chunk].wait_recv()
        side = 0 if chunk < CHUNKS // 2 else 1
        tt_energy = lax.fori_loop(
            chunk * per_chunk, (chunk + 1) * per_chunk, functools.partial(energy, side), tt_energy
        )
    last_sum = Sum(1, sums + (tt_energy,))
    last_sum.start(z_part)
    head_copies = send_heads(0, HALF)
    last_sum.finish()
    last_sum.start(xy_part)
    last_sum.finish()
    rz1, zt, tt, tv, vv, tw, vw, te = last_sum.total()
    beta0 = rz1 / rz0
    alpha1 = jnp.clip(rz1 / (zt - beta0 * rz1 / alpha0), STEP_MIN, STEP_MAX)
    yy = tt + beta0 * (2.0 * tv + beta0 * vv)
    ty = tt + beta0 * tv
    rz2 = jnp.maximum(alpha1 * alpha1 * yy - rz1, 0.0)
    y_energy = te + beta0 * (2.0 * tw + beta0 * vw)
    delta2 = zt - 2.0 * alpha1 * ty + alpha1 * alpha1 * y_energy
    beta1 = rz2 / rz1
    alpha2 = jnp.clip(rz2 / (delta2 - beta1 * rz2 / alpha1), STEP_MIN, STEP_MAX)

    def rim_step(at, side):
        here = rows_at(at)
        z0_rim, z1_rim = z0r[side, here, :], z1r[here, :]
        p1 = z1_rim + beta0 * z0_rim
        z2_rim = z1_rim - alpha1 * (t1r[here, :] + beta0 * v1r[side, here, :])
        return alpha0 * z0_rim + alpha1 * p1 + alpha2 * (z2_rim + beta1 * p1)

    def last_step(i, carry):
        at = pl.multiple_of(i * BLOCK, BLOCK)
        here = rows_at(at)
        there = rows_at(pl.multiple_of(PAD + at, 8))
        z_0, z_1 = zpad[:, there, :], z1[:, here, :]
        p1 = z_1 + beta0 * z_0
        z_2 = z_1 - alpha1 * (tpad[:, there, :] + beta0 * vpad[:, there, :])
        new = alpha0 * z_0 + alpha1 * p1 + alpha2 * (z_2 + beta1 * p1)
        lpad[:, there, :] = new
        adj[:, here, :] = -new
        return carry

    lax.fori_loop(0, ROWS // BLOCK, last_step, 0)

    store = pltpu.make_async_copy(adj, adj_out, local.at[0])
    store.start()
    for copy in head_copies:
        copy.wait_recv()

    def gradient(side, i, carry):
        at = pl.multiple_of(i * BLOCK, BLOCK)
        here = rows_at(at)
        there = rows_at(pl.multiple_of(PAD + at, 8))
        lam = lpad[:, there, :]
        head = hpad[:, there, :]
        lower, upper = rows_at(PAD - 1 + at), rows_at(PAD + 1 + at)
        total = slopes[0, :, here, :] * (lam - lpad[:, lower, :]) * (head - hpad[:, lower, :])
        total = total + slopes[1, :, here, :] * (lam - lpad[:, upper, :]) * (head - hpad[:, upper, :])
        for n, turn in ((2, 1), (3, LANES - 1)):
            total = total + slopes[n, :, here, :] * (lam - pltpu.roll(lam, turn, 2)) * (
                head - pltpu.roll(head, turn, 2)
            )
        across = (lam[0] - lam[1]) * (head[0] - head[1])
        rim = rim_step(at, side)
        over = (lam[side] - rim) * (head[side] - hrim[here, :])
        total0 = total[0] + rim_coef[1, here, :] * across
        total1 = total[1] + rim_coef[2, here, :] * across
        if side == 0:
            total0 = total0 + rim_coef[5, here, :] * over
        else:
            total1 = total1 + rim_coef[6, here, :] * over
        gpart[0, here, :] = total0
        gpart[1, here, :] = total1
        gpart[2, here, :] = rim_coef[7 + side, here, :] * over
        return carry

    blocks = HALF // BLOCK
    lax.fori_loop(0, blocks, functools.partial(gradient, 0), 0)
    lax.fori_loop(blocks, 2 * blocks, functools.partial(gradient, 1), 0)

    other_half = pl.ds(pl.multiple_of((1 - core) * HALF, HALF), HALF)
    quarter = pl.ds(pl.multiple_of(chip * PIECE, PIECE), PIECE)
    parts = (pl.ds(2, 1), pl.ds(0, 2))
    pairs = [begin(gpart.at[part, other_half], pair_in.at[part], test=sibling) for part in parts]
    spread = []
    for part, pair in zip(parts, pairs):
        pair.wait_recv()
        gsum[part] = gpart[part, own_half, :] + pair_in[part]
        spread.append([
            begin(
                gsum.at[part, pl.ds(pl.multiple_of(lax.rem(chip + i + 1, 4) * PIECE, PIECE), PIECE)],
                piece_in.at[i, part], test=mate,
            )
            for i, mate in enumerate(mates)
        ])

    def summed(part):
        return gsum[part, quarter, :] + piece_in[0, part] + piece_in[1, part] + piece_in[2, part]

    for copy in spread[0]:
        copy.wait_recv()
    far_in[pl.ds(0, 1)] = summed(parts[0])
    toward = jnp.where(core == 0, below, above)
    far = begin(far_in.at[0], far_in.at[1], slab=toward)
    for copy in spread[1]:
        copy.wait_recv()
    gfull[:, own, :] = summed(parts[1])
    around = [begin(gfull.at[core, own], gfull.at[core, own], test=mate) for mate in mates]
    far.wait_recv()
    gfull[1 - core, own, :] = gfull[1 - core, own, :] + far_in[1]
    rest = [begin(gfull.at[1 - core, own], gfull.at[1 - core, own], test=mate) for mate in mates]
    for copy in around:
        copy.wait_recv()
    swap = begin(gfull.at[core, own_half], gfull.at[core, own_half], test=sibling)
    for copy in rest:
        copy.wait_recv()
    last = begin(gfull.at[1 - core, own_half], gfull.at[1 - core, own_half], test=sibling)
    swap.wait_recv()
    last.wait_recv()
    result = pltpu.make_async_copy(gfull, grad_out, local.at[1])
    result.start()
    store.wait()
    result.wait()
    for copy in pending:
        copy.wait_send()


def on_device(
    log_conductivity, storage, active_mask, heads, adjoint_next, pump_cells, obs_cells, obs_data
):
    full = (2, ROWS, LANES)
    one = (ROWS, LANES)
    padded = (2, ROWS + 2 * PAD, LANES)
    f32 = lambda *s: pltpu.VMEM(s, jnp.float32)
    anywhere = pl.BlockSpec(memory_space=pl.ANY)
    adjoint, gradient = pl.pallas_call(
        kernel,
        out_shape=[jax.ShapeDtypeStruct(full, jnp.float32)] * 2,
        in_specs=[anywhere] * 8,
        out_specs=[anywhere] * 2,
        scratch_shapes=[
            f32(*full), f32(*full), pltpu.VMEM(full, jnp.int32), f32(*full),
            pltpu.SMEM((1,), jnp.int32), pltpu.VMEM((1, NOBS), jnp.int32), f32(1, NOBS),
            pltpu.SemaphoreType.DMA((8,)),
            f32(*padded), f32(*padded), f32(*padded), f32(*padded),
            f32(*full), f32(*full), f32(4, *full), f32(4, *full), f32(9, *one),
            f32(*full), f32(*full), f32(*full), f32(*full),
            f32(*padded), f32(*padded), f32(*full), f32(*full),
            f32(*full), f32(*full), f32(*one), f32(*one), f32(*one), f32(*one),
            f32(2, 18, 8, LANES), f32(2, 18, 8, LANES),
            f32(3, *one), f32(3, HALF, LANES), f32(3, HALF, LANES), f32(3, 3, PIECE, LANES), f32(*full),
            f32(2, PIECE, LANES),
            pltpu.SemaphoreType.DMA((N_COPIES,)),
            pltpu.SemaphoreType.DMA((N_COPIES,)),
        ],
        compiler_params=pltpu.CompilerParams(
            collective_id=0, has_side_effects=True, vmem_limit_bytes=56 << 20
        ),
    )(
        log_conductivity, storage, active_mask, heads[0], adjoint_next[0], pump_cells,
        obs_cells.reshape(1, NOBS), obs_data,
    )
    return (-adjoint)[None], -gradient


def solution(mesh):
    return jax.shard_map(
        on_device,
        mesh=mesh,
        in_specs=(
            P("slab", None, None),
            P("slab", None, None),
            P("slab", None, None),
            P("test", "slab", None, None),
            P("test", "slab", None, None),
            P("test"),
            P(),
            P("test", None),
        ),
        out_specs=(P("test", "slab", None, None), P("slab", None, None)),
        check_vma=False,
    )
```

```python
import functools

import jax
import jax.numpy as jnp
from jax import lax
from jax.experimental import pallas as pl
from jax.experimental.pallas import tpu as pltpu
from jax.sharding import PartitionSpec as P

MESH = pl.DeviceIdType.MESH
WELL_TERM = 4.0
SLABS = 64
ROWS = 512
LANES = 128
NOBS = 64
PAD = 8
BLOCK = 16
CHUNK = 128
CHUNKS = ROWS // CHUNK
HALF = ROWS // 2
PIECE = 64


class Copies:
    def __init__(self, send, recv):
        self.send, self.recv, self.count = send, recv, 0

    def start(self, src, dst, **where):
        copy = pltpu.make_async_remote_copy(
            src_ref=src,
            dst_ref=dst,
            send_sem=self.send.at[self.count],
            recv_sem=self.recv.at[self.count],
            device_id=where,
            device_id_type=MESH,
        )
        self.count += 1
        copy.start()
        return copy


ORDER = (0, 2, 1, 3)
AHEAD = 2
STAGE = 0
STEP_MIN = 0.5
STEP_MAX = 3400.0
N_COPIES = 2 + 4 + 4 + 2 * CHUNKS + 2 * CHUNKS + CHUNKS + 2 * 18 + 2 + 6 + 1 + 8


def rows_at(start, size=BLOCK):
    return pl.ds(start, size)


def kernel(
    lk_hbm, sto_hbm, act_hbm, hd_hbm, adj_hbm, pump_hbm, cells_hbm, data_hbm, adj_out, grad_out,
    lk, sto, act_in, adj, pump, cells, data, local, kpad, hpad, zpad, lpad, klog, krim, faces, slopes, rim_coef, self_t, diag, inv, rhs,
    vpad, tpad, z1, v2, z0r, v1r, z1r, t1r, v2r, hrim, msg, inbox, gpart, pair_in, gsum, piece_in, gfull,
    far_in, send, recv,
):
    me = lax.axis_index("slab")
    test = lax.axis_index("test")
    above, below = lax.rem(me + 1, SLABS), lax.rem(me + SLABS - 1, SLABS)
    chip, core = test // 2, lax.rem(test, 2)
    sibling = test + 1 - 2 * core
    mates = [lax.rem(test + 2 * i, 8) for i in (1, 2, 3)]
    plane_at, deep = me // 4, lax.rem(me, 4)
    col, line = lax.rem(plane_at, 4), plane_at // 4
    z_part = [plane_at * 4 + lax.rem(deep + i, 4) for i in (1, 2, 3)]
    xy_part = [
        (lax.rem(line + j, 4) * 4 + lax.rem(col + i, 4)) * 4 + deep
        for j in range(4) for i in range(4) if i or j
    ]
    loads = [
        pltpu.make_async_copy(src, dst, local.at[n])
        for n, (src, dst) in enumerate((
            (pump_hbm, pump), (cells_hbm, cells), (data_hbm, data),
            (hd_hbm, hpad.at[:, pl.ds(PAD, ROWS)]), (lk_hbm, lk), (sto_hbm, sto), (act_hbm, act_in),
            (adj_hbm, adj),
        ))
    ]
    barrier = pltpu.get_barrier_semaphore()
    for other in [above, below] + z_part + xy_part:
        pl.semaphore_signal(barrier, inc=1, device_id={"slab": other}, device_id_type=MESH)
    for other in [sibling] + mates:
        pl.semaphore_signal(barrier, inc=1, device_id={"test": other}, device_id_type=MESH)
    for load in loads:
        load.start()
    copies = Copies(send, recv)
    pending = []

    def begin(src, dst, **where):
        copy = copies.start(src, dst, **where)
        pending.append(copy)
        return copy

    own = pl.ds(pl.multiple_of(core * HALF + chip * PIECE, PIECE), PIECE)
    own_half = pl.ds(pl.multiple_of(core * HALF, HALF), HALF)

    pl.semaphore_wait(barrier, 24)
    to_above = begin(lk_hbm.at[1, own], klog.at[0, own], slab=above)
    to_below = begin(lk_hbm.at[0, own], klog.at[1, own], slab=below)

    def send_heads(first, size):
        up, down = pl.ds(first, size), pl.ds(HALF + first, size)
        return [
            begin(hd_hbm.at[1, up], hrim.at[up], slab=above),
            begin(hd_hbm.at[0, down], hrim.at[down], slab=below),
        ]


    low_pad = jnp.zeros((2, PAD, LANES), jnp.float32)
    for ref, fill in ((kpad, 1.0), (hpad, 0.0), (zpad, 0.0), (lpad, 0.0), (vpad, 0.0), (tpad, 0.0)):
        ref[:, pl.ds(0, PAD), :] = low_pad + fill
        ref[:, pl.ds(PAD + ROWS, PAD), :] = low_pad + fill

    for load in loads:
        load.wait()
    offset = me * (2 * ROWS)
    eye = lax.broadcasted_iota(jnp.int32, (NOBS, NOBS), 0) == lax.broadcasted_iota(jnp.int32, (NOBS, NOBS), 1)

    def upright(row):
        return jnp.sum(jnp.where(eye, row, 0.0), axis=1, keepdims=True)

    row_of = cells[...] // LANES
    lane_of = upright((cells[...] - row_of * LANES).astype(jnp.float32))
    row_of = row_of - offset
    cell_row = upright(row_of.astype(jnp.float32))
    lane_index = lax.broadcasted_iota(jnp.int32, (NOBS, LANES), 1).astype(jnp.float32)
    picked = jnp.zeros((NOBS, LANES), jnp.float32)
    for x in range(2):
        index = lax.broadcasted_iota(jnp.int32, (NOBS, ROWS), 1) + x * ROWS
        picked = picked + jnp.dot(
            (index.astype(jnp.float32) == cell_row).astype(jnp.float32), hpad[x, pl.ds(PAD, ROWS), :],
            precision=lax.Precision.HIGHEST, preferred_element_type=jnp.float32,
        )
    values = jnp.where(lane_index == lane_of, picked - upright(data[...]), 0.0)
    for x in range(2):
        index = lax.broadcasted_iota(jnp.int32, (ROWS, NOBS), 0) + x * ROWS
        rhs[x] = jnp.dot(
            (index == row_of).astype(jnp.float32), values,
            precision=lax.Precision.HIGHEST, preferred_element_type=jnp.float32,
        )

    well_at = pump[0] - offset * LANES
    shape = (2, BLOCK, LANES)
    lane_no = lax.broadcasted_iota(jnp.int32, shape, 2)
    row_no = lax.broadcasted_iota(jnp.int32, shape, 1)
    cell_no = lax.broadcasted_iota(jnp.int32, shape, 0) * (ROWS * LANES) + row_no * LANES + lane_no

    def prepare(i, carry):
        at = pl.multiple_of(i * BLOCK, BLOCK)
        here = rows_at(at)
        kpad[:, rows_at(pl.multiple_of(PAD + at, 8)), :] = jnp.exp(lk[:, here, :])
        return carry

    lax.fori_loop(0, ROWS // BLOCK, prepare, 0)

    def local_terms(i, carry):
        at = pl.multiple_of(i * BLOCK, BLOCK)
        here = rows_at(at)
        k = kpad[:, rows_at(pl.multiple_of(PAD + at, 8)), :]
        total = jnp.zeros(shape, jnp.float32)
        sides = (
            (kpad[:, rows_at(PAD - 1 + at), :], row_no + at > 0),
            (kpad[:, rows_at(PAD + 1 + at), :], row_no + at < ROWS - 1),
            (pltpu.roll(k, 1, 2), lane_no > 0),
            (pltpu.roll(k, LANES - 1, 2), lane_no < LANES - 1),
        )
        for n, (other, inside) in enumerate(sides):
            both = k + other
            face = jnp.where(inside, 2.0 * k * other / both, 0.0)
            faces[n, :, here, :] = face
            slopes[n, :, here, :] = face * other / both
            total = total + face
        both = k[0] + k[1]
        face = 2.0 * k[0] * k[1] / both
        rim_coef[0, here, :] = face
        rim_coef[1, here, :] = face * k[1] / both
        rim_coef[2, here, :] = face * k[0] / both
        well = jnp.where(cell_no + at * LANES == well_at, WELL_TERM, 0.0)
        self_here = sto[:, here, :] + well
        self_t[:, here, :] = self_here
        diag[:, here, :] = self_here + total + face[None]
        active = act_in[:, here, :].astype(jnp.float32)
        rhs[:, here, :] = active * (sto[:, here, :] * adj[:, here, :] + rhs[:, here, :])
        return carry

    lax.fori_loop(0, ROWS // BLOCK, local_terms, 0)

    def gather(ref, arrived):
        for copy in arrived:
            copy.wait_recv()
        around = [begin(ref.at[:, own], ref.at[:, own], test=mate) for mate in mates]
        for copy in around:
            copy.wait_recv()
        begin(ref.at[:, own_half], ref.at[:, own_half], test=sibling).wait_recv()

    gather(klog, [to_above, to_below])

    low_edge = jnp.where(me > 0, 1.0, 0.0)
    high_edge = jnp.where(me < SLABS - 1, 1.0, 0.0)

    def rim_terms(i, carry):
        at = pl.multiple_of(i * BLOCK, BLOCK)
        here = rows_at(at)
        k = kpad[:, rows_at(pl.multiple_of(PAD + at, 8)), :]
        other = jnp.exp(klog[:, here, :])
        krim[:, here, :] = other
        both = k + other
        face = 2.0 * k * other / both
        low = face[0] * low_edge
        high = face[1] * high_edge
        rim_coef[3, here, :] = low
        rim_coef[4, here, :] = high
        rim_coef[5, here, :] = low * other[0] / both[0]
        rim_coef[6, here, :] = high * other[1] / both[1]
        rim_coef[7, here, :] = low * k[0] / both[0]
        rim_coef[8, here, :] = high * k[1] / both[1]
        active = act_in[:, here, :].astype(jnp.float32)
        fixed = 1.0 - active
        d0 = active[0] * (diag[0, here, :] + low) + fixed[0]
        d1 = active[1] * (diag[1, here, :] + high) + fixed[1]
        diag[0, here, :] = d0
        diag[1, here, :] = d1
        inv[0, here, :] = 1.0 / d0
        inv[1, here, :] = 1.0 / d1
        there = rows_at(pl.multiple_of(PAD + at, 8))
        z0 = rhs[0, here, :] / d0
        z1 = rhs[1, here, :] / d1
        zpad[0, there, :] = z0
        zpad[1, there, :] = z1
        return carry

    def send_rims(ref, pad, rims, chunk):
        src = pl.ds(pad + chunk * CHUNK, CHUNK)
        dst = pl.ds(chunk * CHUNK, CHUNK)
        return [
            begin(ref.at[1, src], rims.at[0, dst], slab=above),
            begin(ref.at[0, src], rims.at[1, dst], slab=below),
        ]

    per_chunk = CHUNK // BLOCK
    z_copies = {}
    for chunk in ORDER:
        lax.fori_loop(chunk * per_chunk, (chunk + 1) * per_chunk, rim_terms, 0)
        z_copies[chunk] = send_rims(zpad, PAD, z0r, chunk)

    def image_of(ref, at, rim_low, rim_high):
        here = rows_at(at)
        z = ref[:, rows_at(pl.multiple_of(PAD + at, 8)), :]
        flux = faces[0, :, here, :] * (z - ref[:, rows_at(PAD - 1 + at), :])
        flux = flux + faces[1, :, here, :] * (z - ref[:, rows_at(PAD + 1 + at), :])
        flux = flux + faces[2, :, here, :] * (z - pltpu.roll(z, 1, 2))
        flux = flux + faces[3, :, here, :] * (z - pltpu.roll(z, LANES - 1, 2))
        across = rim_coef[0, here, :] * (z[0] - z[1])
        low = across + rim_coef[3, here, :] * (z[0] - rim_low)
        high = rim_coef[4, here, :] * (z[1] - rim_high) - across
        active = act_in[:, here, :].astype(jnp.float32)
        body = self_t[:, here, :] * z + flux
        image0 = active[0] * (body[0] + low) + (1.0 - active[0]) * z[0]
        image1 = active[1] * (body[1] + high) + (1.0 - active[1]) * z[1]
        return z, image0, image1

    zero = jnp.zeros((BLOCK, LANES), jnp.float32)

    class Sum:
        def __init__(self, which, sums):
            rows = [jnp.sum(s, axis=0, keepdims=True) for s in sums]
            rows = rows + [jnp.zeros((1, LANES), jnp.float32)] * (8 - len(rows))
            self.which, self.n, self.value = which, 0, jnp.concatenate(rows, axis=0)

        def start(self, stage):
            msg[self.which, self.n] = self.value
            self.batch = [
                begin(msg.at[self.which, self.n], inbox.at[self.which, self.n + i], slab=other)
                for i, other in enumerate(stage)
            ]

        def finish(self):
            for copy in self.batch:
                copy.wait_recv()
            for i in range(len(self.batch)):
                self.value = self.value + inbox[self.which, self.n + i]
            self.n += len(self.batch)

        def total(self):
            total = jnp.broadcast_to(jnp.sum(self.value, axis=1, keepdims=True), (8, LANES))
            return [total[i:i + 1] for i in range(8)]

    def first_image(i, sums):
        at = pl.multiple_of(i * BLOCK, BLOCK)
        here = rows_at(at)
        there = rows_at(pl.multiple_of(PAD + at, 8))
        z, image0, image1 = image_of(zpad, at, z0r[0, here, :], z0r[1, here, :])
        vpad[0, there, :] = image0 * inv[0, here, :]
        vpad[1, there, :] = image1 * inv[1, here, :]
        d = diag[:, here, :]
        rz = sums[0] + z[0] * z[0] * d[0] + z[1] * z[1] * d[1]
        return rz, sums[1] + z[0] * image0 + z[1] * image1

    sums = (zero, zero)
    v1_copies = {}

    def send_v1(chunks):
        for chunk in chunks:
            v1_copies[chunk] = send_rims(vpad, PAD, v1r, chunk)

    for n, chunk in enumerate(ORDER):
        for copy in z_copies[chunk]:
            copy.wait_recv()
        sums = lax.fori_loop(chunk * per_chunk, (chunk + 1) * per_chunk, first_image, sums)
        if n < AHEAD:
            send_v1([chunk])
    first_sum = Sum(0, sums)
    first_sum.start(z_part)
    send_v1(ORDER[AHEAD:])

    def second_image(i, carry):
        at = pl.multiple_of(i * BLOCK, BLOCK)
        here = rows_at(at)
        _, image0, image1 = image_of(vpad, at, v1r[0, here, :], v1r[1, here, :])
        v2[0, here, :] = image0 * inv[0, here, :]
        v2[1, here, :] = image1 * inv[1, here, :]
        return carry

    v2_copies = {}
    for n, chunk in enumerate(ORDER):
        for copy in v1_copies[chunk]:
            copy.wait_recv()
        lax.fori_loop(chunk * per_chunk, (chunk + 1) * per_chunk, second_image, 0)
        part = pl.ds(chunk * CHUNK, CHUNK)
        if chunk < CHUNKS // 2:
            v2_copies[chunk] = begin(v2.at[1, part], v2r.at[part], slab=above)
        else:
            v2_copies[chunk] = begin(v2.at[0, part], v2r.at[part], slab=below)
        if n == STAGE:
            first_sum.finish()
            first_sum.start(xy_part)
    first_sum.finish()
    rz0, pw0 = first_sum.total()[:2]
    alpha0 = jnp.clip(rz0 / pw0, STEP_MIN, STEP_MAX)

    def step_one(i, sums):
        at = pl.multiple_of(i * BLOCK, BLOCK)
        here = rows_at(at)
        there = rows_at(pl.multiple_of(PAD + at, 8))
        v_one = vpad[:, there, :]
        v_two = v2[:, here, :]
        z_new = zpad[:, there, :] - alpha0 * v_one
        t_new = v_one - alpha0 * v_two
        z1[:, here, :] = z_new
        tpad[:, there, :] = t_new
        d = diag[:, here, :]
        z_d, t_d, v_d = z_new * d, t_new * d, v_one * d
        terms = (
            z_d * z_new, z_d * t_new, t_d * t_new, t_d * v_one, v_d * v_one, t_d * v_two, v_d * v_two,
        )
        return tuple(s + term[0] + term[1] for s, term in zip(sums, terms))

    sums = lax.fori_loop(0, ROWS // BLOCK, step_one, (zero,) * 7)

    def energy(side, i, total):
        at = pl.multiple_of(i * BLOCK, BLOCK)
        here = rows_at(at)
        t = tpad[:, rows_at(pl.multiple_of(PAD + at, 8)), :]
        v_rim = v1r[side, here, :]
        rim = v_rim - alpha0 * v2r[here, :]
        t1r[here, :] = rim
        z1r[here, :] = z0r[side, here, :] - alpha0 * v_rim
        up = t - tpad[:, rows_at(PAD + 1 + at), :]
        right = t - pltpu.roll(t, LANES - 1, 2)
        across = t[0] - t[1]
        over = t[side] - rim
        square = faces[1, :, here, :] * up * up + faces[3, :, here, :] * right * right
        square = square + self_t[:, here, :] * t * t
        active = act_in[:, here, :].astype(jnp.float32)
        square = square + (1.0 - active) * t * t
        total = total + square[0] + square[1] + rim_coef[0, here, :] * across * across
        return total + rim_coef[3 + side, here, :] * over * over

    tt_energy = zero
    for chunk in ORDER:
        v2_copies[chunk].wait_recv()
        side = 0 if chunk < CHUNKS // 2 else 1
        tt_energy = lax.fori_loop(
            chunk * per_chunk, (chunk + 1) * per_chunk, functools.partial(energy, side), tt_energy
        )
    last_sum = Sum(1, sums + (tt_energy,))
    last_sum.start(z_part)
    head_copies = send_heads(0, HALF // 2)
    last_sum.finish()
    last_sum.start(xy_part)
    head_copies = head_copies + send_heads(HALF // 2, HALF // 2)
    last_sum.finish()
    rz1, zt, tt, tv, vv, tw, vw, te = last_sum.total()
    beta0 = rz1 / rz0
    alpha1 = jnp.clip(rz1 / (zt - beta0 * rz1 / alpha0), STEP_MIN, STEP_MAX)
    yy = tt + beta0 * (2.0 * tv + beta0 * vv)
    ty = tt + beta0 * tv
    rz2 = jnp.maximum(alpha1 * alpha1 * yy - rz1, 0.0)
    y_energy = te + beta0 * (2.0 * tw + beta0 * vw)
    delta2 = zt - 2.0 * alpha1 * ty + alpha1 * alpha1 * y_energy
    beta1 = rz2 / rz1
    alpha2 = jnp.clip(rz2 / (delta2 - beta1 * rz2 / alpha1), STEP_MIN, STEP_MAX)

    def rim_step(at, side):
        here = rows_at(at)
        z0_rim, z1_rim = z0r[side, here, :], z1r[here, :]
        p1 = z1_rim + beta0 * z0_rim
        z2_rim = z1_rim - alpha1 * (t1r[here, :] + beta0 * v1r[side, here, :])
        return alpha0 * z0_rim + alpha1 * p1 + alpha2 * (z2_rim + beta1 * p1)

    def last_step(i, carry):
        at = pl.multiple_of(i * BLOCK, BLOCK)
        here = rows_at(at)
        there = rows_at(pl.multiple_of(PAD + at, 8))
        z_0, z_1 = zpad[:, there, :], z1[:, here, :]
        p1 = z_1 + beta0 * z_0
        z_2 = z_1 - alpha1 * (tpad[:, there, :] + beta0 * vpad[:, there, :])
        new = alpha0 * z_0 + alpha1 * p1 + alpha2 * (z_2 + beta1 * p1)
        lpad[:, there, :] = new
        adj[:, here, :] = -new
        return carry

    lax.fori_loop(0, ROWS // BLOCK, last_step, 0)

    store = pltpu.make_async_copy(adj, adj_out, local.at[0])
    store.start()
    for copy in head_copies:
        copy.wait_recv()

    def gradient(side, i, carry):
        at = pl.multiple_of(i * BLOCK, BLOCK)
        here = rows_at(at)
        there = rows_at(pl.multiple_of(PAD + at, 8))
        lam = lpad[:, there, :]
        head = hpad[:, there, :]
        lower, upper = rows_at(PAD - 1 + at), rows_at(PAD + 1 + at)
        total = slopes[0, :, here, :] * (lam - lpad[:, lower, :]) * (head - hpad[:, lower, :])
        total = total + slopes[1, :, here, :] * (lam - lpad[:, upper, :]) * (head - hpad[:, upper, :])
        for n, turn in ((2, 1), (3, LANES - 1)):
            total = total + slopes[n, :, here, :] * (lam - pltpu.roll(lam, turn, 2)) * (
                head - pltpu.roll(head, turn, 2)
            )
        across = (lam[0] - lam[1]) * (head[0] - head[1])
        rim = rim_step(at, side)
        over = (lam[side] - rim) * (head[side] - hrim[here, :])
        total0 = total[0] + rim_coef[1, here, :] * across
        total1 = total[1] + rim_coef[2, here, :] * across
        if side == 0:
            total0 = total0 + rim_coef[5, here, :] * over
        else:
            total1 = total1 + rim_coef[6, here, :] * over
        gpart[0, here, :] = total0
        gpart[1, here, :] = total1
        gpart[2, here, :] = rim_coef[7 + side, here, :] * over
        return carry

    blocks = HALF // BLOCK
    lax.fori_loop(0, blocks, functools.partial(gradient, 0), 0)
    lax.fori_loop(blocks, 2 * blocks, functools.partial(gradient, 1), 0)

    other_half = pl.ds(pl.multiple_of((1 - core) * HALF, HALF), HALF)
    quarter = pl.ds(pl.multiple_of(chip * PIECE, PIECE), PIECE)
    parts = (pl.ds(2, 1), pl.ds(0, 2))
    pairs = [begin(gpart.at[part, other_half], pair_in.at[part], test=sibling) for part in parts]
    spread = []
    for part, pair in zip(parts, pairs):
        pair.wait_recv()
        gsum[part] = gpart[part, own_half, :] + pair_in[part]
        spread.append([
            begin(
                gsum.at[part, pl.ds(pl.multiple_of(lax.rem(chip + i + 1, 4) * PIECE, PIECE), PIECE)],
                piece_in.at[i, part], test=mate,
            )
            for i, mate in enumerate(mates)
        ])

    def summed(part):
        return gsum[part, quarter, :] + piece_in[0, part] + piece_in[1, part] + piece_in[2, part]

    for copy in spread[0]:
        copy.wait_recv()
    far_in[pl.ds(0, 1)] = summed(parts[0])
    toward = jnp.where(core == 0, below, above)
    far = begin(far_in.at[0], far_in.at[1], slab=toward)
    for copy in spread[1]:
        copy.wait_recv()
    gfull[:, own, :] = summed(parts[1])
    around = [begin(gfull.at[core, own], gfull.at[core, own], test=mate) for mate in mates]
    far.wait_recv()
    gfull[1 - core, own, :] = gfull[1 - core, own, :] + far_in[1]
    rest = [begin(gfull.at[1 - core, own], gfull.at[1 - core, own], test=mate) for mate in mates]
    for copy in around:
        copy.wait_recv()
    swap = begin(gfull.at[core, own_half], gfull.at[core, own_half], test=sibling)
    for copy in rest:
        copy.wait_recv()
    last = begin(gfull.at[1 - core, own_half], gfull.at[1 - core, own_half], test=sibling)
    swap.wait_recv()
    last.wait_recv()
    result = pltpu.make_async_copy(gfull, grad_out, local.at[1])
    result.start()
    store.wait()
    result.wait()
    for copy in pending:
        copy.wait_send()


def on_device(
    log_conductivity, storage, active_mask, heads, adjoint_next, pump_cells, obs_cells, obs_data
):
    full = (2, ROWS, LANES)
    one = (ROWS, LANES)
    padded = (2, ROWS + 2 * PAD, LANES)
    f32 = lambda *s: pltpu.VMEM(s, jnp.float32)
    anywhere = pl.BlockSpec(memory_space=pl.ANY)
    adjoint, gradient = pl.pallas_call(
        kernel,
        out_shape=[jax.ShapeDtypeStruct(full, jnp.float32)] * 2,
        in_specs=[anywhere] * 8,
        out_specs=[anywhere] * 2,
        scratch_shapes=[
            f32(*full), f32(*full), pltpu.VMEM(full, jnp.int32), f32(*full),
            pltpu.SMEM((1,), jnp.int32), pltpu.VMEM((1, NOBS), jnp.int32), f32(1, NOBS),
            pltpu.SemaphoreType.DMA((8,)),
            f32(*padded), f32(*padded), f32(*padded), f32(*padded),
            f32(*full), f32(*full), f32(4, *full), f32(4, *full), f32(9, *one),
            f32(*full), f32(*full), f32(*full), f32(*full),
            f32(*padded), f32(*padded), f32(*full), f32(*full),
            f32(*full), f32(*full), f32(*one), f32(*one), f32(*one), f32(*one),
            f32(2, 18, 8, LANES), f32(2, 18, 8, LANES),
            f32(3, *one), f32(3, HALF, LANES), f32(3, HALF, LANES), f32(3, 3, PIECE, LANES), f32(*full),
            f32(2, PIECE, LANES),
            pltpu.SemaphoreType.DMA((N_COPIES,)),
            pltpu.SemaphoreType.DMA((N_COPIES,)),
        ],
        compiler_params=pltpu.CompilerParams(
            collective_id=0, has_side_effects=True, vmem_limit_bytes=56 << 20
        ),
    )(
        log_conductivity, storage, active_mask, heads[0], adjoint_next[0], pump_cells,
        obs_cells.reshape(1, NOBS), obs_data,
    )
    return (-adjoint)[None], -gradient


def solution(mesh):
    return jax.shard_map(
        on_device,
        mesh=mesh,
        in_specs=(
            P("slab", None, None),
            P("slab", None, None),
            P("slab", None, None),
            P("test", "slab", None, None),
            P("test", "slab", None, None),
            P("test"),
            P(),
            P("test", None),
        ),
        out_specs=(P("test", "slab", None, None), P("slab", None, None)),
        check_vma=False,
    )
```
